512 devices in a mesh: section: 16 (over y, z_hi), inst: 4 (over x), tp: 8 (over z_lo, core).
Axes of the slice: x: 4, y: 8, z: 8 (z_hi: 2, z_lo: 4; z = z_hi * 4 + z_lo), core: 2. Of those that a mesh axis runs over, the one named last changes fastest.
Arguments:
- queries: bfloat16 [16, 128, 8192], P('section', 'inst', 'tp'), may hold values from -8 to 8
- new_kv: bfloat16 [16, 128, 2, 1024], P('section', 'inst', None, 'tp'), may hold values from -8 to 8
- kv_pages: bfloat16 [16, 512, 2, 64, 1024], P('section', 'inst', None, None, 'tp'), may hold values from -8 to 8
- lengths: int32 [16, 128], P('section'), may hold values from 1 to 448, as said below
- block_tables: int32 [16, 128, 7], P('section'), may hold values from 0 to 511, as said below
Outputs:
- attended: bfloat16 [16, 128, 8192], P('section', ('inst', 'tp'))
The draws below stay inside these ranges and needn't reach their ends.
Inputs may be any that keep to these rules, and one draw needn't show every extreme that they name: `lengths`: some row of every layer has 448 tokens. `block_tables`: page p lies in the pool of instance p // 128. The pages that the rows of one layer use (positions k below ceil(lengths / 64)) are all different; entries at later positions are arbitrary page numbers.
All inputs are finite; a program needn't handle non-finite values.
Results may differ from the reference program's by a relative error of at most 0.0028.
Values may be sent and summed in bfloat16 or wider, within the bound.
A program may use at most 64 MiB of HBM per device.

```python
import math
import jax
import jax.numpy as jnp
from jax import lax

HEADS = 64
KV_HEADS = 8
HEAD_DIM = 128
PAGE = 64
MAXP = 7
LAYERS = 16
ROWS = 128
PAGES = 512


def layer_permutation(layer_key, count):
    return jax.random.permutation(layer_key, count)


def page_plan(key):
    key = jax.random.fold_in(key, 101)
    key_first, key_second, key_order, key_tail, key_slots, key_filler = jax.random.split(key, 6)
    half_rows = ROWS // 2
    first_count = jax.random.randint(key_first, (LAYERS, half_rows), 1, MAXP + 1)
    first_count = first_count.at[:, 0].set(MAXP)
    second_raw = jax.random.randint(key_second, (LAYERS, half_rows), 0, MAXP + 1)
    second_count = 1 + second_raw % (MAXP + 1 - first_count)
    paired = jnp.stack([first_count, second_count], axis=2).reshape(LAYERS, ROWS)
    forced = jnp.zeros((LAYERS, ROWS), jnp.int32).at[:, 0].set(1)
    orders = jax.vmap(lambda layer_key: layer_permutation(layer_key, ROWS))(jax.random.split(key_order, LAYERS))
    counts = jnp.take_along_axis(paired, orders, axis=1)
    forced = jnp.take_along_axis(forced, orders, axis=1)
    tails = jax.random.randint(key_tail, (LAYERS, ROWS), 1, PAGE + 1)
    tails = jnp.where(forced > 0, PAGE, tails)
    row_lengths = (counts - 1) * PAGE + tails
    slots = jax.vmap(lambda layer_key: layer_permutation(layer_key, PAGES))(jax.random.split(key_slots, LAYERS))
    offsets = jnp.cumsum(counts, axis=1) - counts
    page_number = jnp.arange(MAXP, dtype=jnp.int32)
    slot_index = jnp.minimum(offsets[:, :, None] + page_number[None, None, :], PAGES - 1)
    chosen = jnp.take_along_axis(slots, slot_index.reshape(LAYERS, ROWS * MAXP), axis=1).reshape(LAYERS, ROWS, MAXP)
    filler = jax.random.randint(key_filler, (LAYERS, ROWS, MAXP), 0, PAGES)
    tables = jnp.where(page_number[None, None, :] < counts[:, :, None], chosen, filler)
    return (row_lengths.astype(jnp.int32), tables.astype(jnp.int32))


def draw_lengths(key, part):
    row_lengths, tables = page_plan(key)
    return row_lengths


def draw_block_tables(key, part):
    row_lengths, tables = page_plan(key)
    return tables


def draw_queries(key, part):
    key = jax.random.fold_in(key, 11)
    key_noise = jax.random.fold_in(key, 0)
    noise_part = jax.random.normal(key_noise, (LAYERS, ROWS, HEADS, HEAD_DIM), jnp.float32)
    values = noise_part
    values = jnp.clip(values, -8.0, 8.0)
    return values.reshape(LAYERS, ROWS, HEADS * HEAD_DIM).astype(jnp.bfloat16)


def draw_new_kv(key, part):
    key = jax.random.fold_in(key, 17)
    key_noise = jax.random.fold_in(key, 0)
    noise_part = jax.random.normal(key_noise, (LAYERS, ROWS, 2, KV_HEADS, HEAD_DIM), jnp.float32)
    key_mask = (jnp.arange(2) == 0).reshape(1, 1, 2, 1, 1)
    values = jnp.where(key_mask, 3.0 * noise_part, noise_part)
    values = jnp.clip(values, -8.0, 8.0)
    return values.reshape(LAYERS, ROWS, 2, KV_HEADS * HEAD_DIM).astype(jnp.bfloat16)


def draw_kv_pages(key, part):
    key = jax.random.fold_in(key, 13)
    key_noise = jax.random.fold_in(key, 0)
    full_shape = (LAYERS, PAGES, 2, PAGE, KV_HEADS, HEAD_DIM)
    noise_part = jax.random.normal(key_noise, full_shape, jnp.float32)
    values = noise_part
    values = jnp.clip(values, -8.0, 8.0)
    return values.reshape(LAYERS, PAGES, 2, PAGE, KV_HEADS * HEAD_DIM).astype(jnp.bfloat16)


def setup_inputs(seed: int = 0) -> dict:
    splits = jax.random.split(jax.random.key(seed), 6)
    return {
        "queries": draw_queries(jax.random.fold_in(splits[5], 71), 0),
        "new_kv": draw_new_kv(jax.random.fold_in(splits[5], 71), 0),
        "kv_pages": draw_kv_pages(jax.random.fold_in(splits[5], 71), 0),
        "lengths": draw_lengths(jax.random.fold_in(splits[5], 71), 0),
        "block_tables": draw_block_tables(jax.random.fold_in(splits[5], 71), 0),
    }


NEGATIVE = -1e+30

def layer_attention(operands):
    layer_query, layer_fresh, layer_pages, layer_length, layer_table = operands
    score_scale = 1.0 / math.sqrt(HEAD_DIM)
    head_group = HEADS // KV_HEADS
    query_float = layer_query.astype(jnp.float32).reshape(ROWS, KV_HEADS, head_group, HEAD_DIM)
    picked = jnp.take(layer_pages, layer_table, axis=0)
    page_keys = picked[:, :, 0].astype(jnp.float32).reshape(ROWS, MAXP, PAGE, KV_HEADS, HEAD_DIM)
    page_values = picked[:, :, 1].astype(jnp.float32).reshape(ROWS, MAXP, PAGE, KV_HEADS, HEAD_DIM)
    scores = jnp.einsum('rhgd,rkjhd->rkhgj', query_float, page_keys) * score_scale
    positions = jnp.arange(MAXP, dtype=jnp.int32)[:, None] * PAGE + jnp.arange(PAGE, dtype=jnp.int32)[None, :]
    token_valid = (positions[None] < layer_length[:, None, None])[:, :, None, None, :]
    scores = jnp.where(token_valid, scores, NEGATIVE)
    page_max = lax.optimization_barrier(jnp.max(scores, axis=-1))
    weights = jnp.where(token_valid, jnp.exp(scores - page_max[..., None]), 0.0)
    page_sum = lax.optimization_barrier(jnp.sum(weights, axis=-1))
    rounded = lax.optimization_barrier(weights.astype(jnp.bfloat16)).astype(jnp.float32)
    page_out = jnp.einsum('rkhgj,rkjhd->rkhgd', rounded, page_values)
    own_key = layer_fresh[:, 0].astype(jnp.float32).reshape(ROWS, KV_HEADS, HEAD_DIM)
    own_value = layer_fresh[:, 1].astype(jnp.float32).reshape(ROWS, KV_HEADS, HEAD_DIM)
    own_score = jnp.einsum('rhgd,rhd->rhg', query_float, own_key) * score_scale
    highest = jnp.maximum(own_score, lax.optimization_barrier(jnp.max(page_max, axis=1)))
    own_weight = jnp.exp(own_score - highest)
    page_factor = jnp.exp(page_max - highest[:, None])
    denominator = own_weight + lax.optimization_barrier(jnp.sum(page_factor * page_sum, axis=1))
    combined = own_weight[..., None] * own_value[:, :, None, :] + lax.optimization_barrier(jnp.sum(page_factor[..., None] * page_out, axis=1))
    result = combined / denominator[..., None]
    return result.reshape(ROWS, HEADS * HEAD_DIM).astype(jnp.bfloat16)

def reference(queries, new_kv, kv_pages, lengths, block_tables):
    section_result = lax.map(layer_attention, (queries, new_kv, kv_pages, lengths, block_tables))
    return jnp.roll(section_result, 1, axis=0)
```

```python
import functools
import math

import jax
import jax.numpy as jnp
from jax import lax
from jax.experimental import pallas as pl
from jax.experimental.pallas import tpu as pltpu
from jax.sharding import PartitionSpec as P

HEAD_DIM = 128
NEGATIVE = -1e30
GROUP = 8
MESH = pl.DeviceIdType.MESH
F32 = jnp.float32
BF16 = jnp.bfloat16


def iota(shape, dim):
    return lax.broadcasted_iota(jnp.int32, shape, dim)


def dot(a, b):
    return lax.dot_general(a, b, (((1,), (0,)), ((), ())), preferred_element_type=F32)


def dot_nt(a, b):
    return lax.dot_general(a, b, (((1,), (1,)), ((), ())), preferred_element_type=F32)


def split(x):
    high = x.astype(BF16)
    return high, (x - high.astype(F32)).astype(BF16)


def kernel(
    sizes,
    q_hbm,
    fresh_hbm,
    kv_hbm,
    len_hbm,
    table_hbm,
    out_ref,
    q_all,
    fresh,
    fresh_f,
    kv,
    length,
    table,
    page_x,
    page_m,
    page_s,
    p_send,
    p_recv,
    r_send,
    load_sem,
    kv_sem,
    q_ssem,
    q_rsem,
    p_ssem,
    p_rsem,
    r_ssem,
    r_rsem,
):
    sections, insts, tps, home, pool, slots, page, heads = sizes
    rows = home * insts
    part = home // tps
    scale = 1.0 / math.sqrt(HEAD_DIM)
    sec = lax.axis_index("section")
    me = lax.axis_index("inst")
    tp = lax.axis_index("tp")
    my_rows = pl.ds(pl.multiple_of(me * home, home), home)

    load_q = pltpu.make_async_copy(q_hbm, q_all.at[my_rows], load_sem.at[0])
    load_fresh = pltpu.make_async_copy(fresh_hbm, fresh, load_sem.at[1])
    load_len = pltpu.make_async_copy(len_hbm, length, load_sem.at[2])
    load_table = pltpu.make_async_copy(table_hbm, table, load_sem.at[3])
    load_q.start()
    load_table.start()
    load_len.start()
    load_fresh.start()

    barrier = pltpu.get_barrier_semaphore()
    for o in range(1, insts):
        pl.semaphore_signal(
            barrier, inc=1, device_id={"inst": lax.rem(me + o, insts)}, device_id_type=MESH
        )
    before = lax.rem(sec + sections - 1, sections)
    after = lax.rem(sec + 1, sections)
    for t in range(tps):
        pl.semaphore_signal(
            barrier, inc=1, device_id={"section": before, "tp": t}, device_id_type=MESH
        )
    chunks = kv_sem.shape[0]
    per = pool // chunks
    load_kv = [
        pltpu.make_async_copy(
            kv_hbm.at[pl.ds(c * per, per)], kv.at[pl.ds(c * per, per)], kv_sem.at[c]
        )
        for c in range(chunks)
    ]
    for copy in load_kv:
        copy.start()

    load_q.wait()
    pl.semaphore_wait(barrier, insts - 1 + tps)

    q_copies = []
    for o in (2, 1, 3):
        copy = pltpu.make_async_remote_copy(
            src_ref=q_all.at[my_rows],
            dst_ref=q_all.at[my_rows],
            send_sem=q_ssem.at[o - 1],
            recv_sem=q_rsem.at[o - 1],
            device_id={"inst": lax.rem(me + o, insts)},
            device_id_type=MESH,
        )
        copy.start()
        q_copies.append(copy)

    load_len.wait()
    load_table.wait()
    page_id = iota((pool, rows), 0)
    counted = jnp.zeros((pool, rows), jnp.int32)
    for k in range(slots):
        local = table[k] - me * pool
        live = jnp.clip(length[...] - k * page, 0, page)
        counted = counted + jnp.where(page_id == local, live, 0)
    owned = counted > 0
    owner_f = jnp.where(owned, 1.0, 0.0).astype(F32)
    owner = owner_f.astype(BF16)
    owner_t = owner_f.T.astype(BF16)
    owner_t2 = jnp.concatenate([owner_t, owner_t], axis=1)
    tokens = dot(counted.astype(F32).astype(BF16), jnp.ones((rows, 128), BF16))

    load_fresh.wait()
    fresh_f[...] = fresh[...].astype(F32)
    own_k = fresh_f[pl.ds(0, home, stride=2), :]
    own_v = fresh_f[pl.ds(1, home, stride=2), :]
    lane = iota((home, 128), 1)
    own = jnp.zeros((home, 128), F32)
    q_mine = q_all[my_rows, :].astype(F32)
    for h in range(heads):
        score = jnp.sum(q_mine[:, h * 128 : (h + 1) * 128] * own_k, axis=1, keepdims=True) * scale
        own = jnp.where(lane == h, score, own)

    for copy in q_copies:
        copy.wait_recv()
    picked = dot(owner, q_all[...])
    for copy in load_kv:
        copy.wait()

    stack = heads * GROUP
    row_page = lax.rem(iota((stack, 128), 0), GROUP)
    per_tile = 128 // page
    tiles = GROUP // per_tile
    tile_of = row_page // per_tile
    token = iota((stack, 128), 1) - lax.rem(row_page, per_tile) * page
    token_f = token.astype(F32)
    for g in range(pool // GROUP):
        at = slice(g * GROUP, (g + 1) * GROUP)
        group_q = jnp.concatenate(
            [picked[at, h * 128 : (h + 1) * 128] for h in range(heads)], axis=0
        ).astype(BF16)
        keys = kv[at, 0].reshape(GROUP * page, 128)
        values = kv[at, 1].reshape(GROUP * page, 128)
        full = dot_nt(group_q, keys)
        scores = full[:, :128]
        for c in range(1, tiles):
            scores = jnp.where(tile_of == c, full[:, c * 128 : (c + 1) * 128], scores)
        limit = jnp.concatenate([tokens[at]] * heads, axis=0)
        valid = (token >= 0) & (token_f < limit)
        scores = jnp.where(valid, scores * scale, NEGATIVE)
        highest = jnp.max(scores, axis=1, keepdims=True)
        weights = jnp.where(valid, jnp.exp(scores - highest), 0.0)
        total = jnp.sum(weights, axis=1, keepdims=True)
        spread = jnp.concatenate(
            [jnp.where(tile_of == c, weights, 0.0).astype(BF16) for c in range(tiles)], axis=1
        )
        x = dot(spread, values)
        page_x[:, at, :] = x.reshape(heads, GROUP, 128)
        page_m[:, at, :] = jnp.broadcast_to(highest, (stack, 128)).reshape(heads, GROUP, 128)
        page_s[:, at, :] = jnp.broadcast_to(total, (stack, 128)).reshape(heads, GROUP, 128)

    refs = []
    for h in range(heads):
        rounded = page_m[h].astype(BF16).astype(F32)
        refs.append(jnp.max(jnp.where(owned, rounded, NEGATIVE), axis=0, keepdims=True))
    sums = jnp.zeros((pool, 128), F32)
    pool_lane = iota((pool, 128), 1)
    for h in range(0, heads, 2):
        sides = []
        for j in (h, h + 1):
            page_ref = dot_nt(owner, jnp.broadcast_to(refs[j], (128, rows)).astype(BF16))
            factor = jnp.exp(page_m[j] - page_ref)
            sums = jnp.where(pool_lane == heads + j, factor * page_s[j], sums)
            high, low = split(factor * page_x[j])
            sides.append(jnp.concatenate([high, low], axis=0))
        both = dot(owner_t2, jnp.concatenate(sides, axis=1))
        for d in range(insts):
            for j in range(2):
                p_send[d, (h + j) * home : (h + j + 1) * home, :] = both[
                    d * home : (d + 1) * home, j * 128 : (j + 1) * 128
                ]
    high, low = split(sums)
    stat = dot(owner_t2, jnp.concatenate([high, low], axis=0))
    ref_pad = jnp.concatenate(refs + [jnp.zeros((128 - heads, rows), F32)], axis=0)
    stat = stat + ref_pad.T
    for d in range(insts):
        p_send[d, heads * home :, :] = stat[d * home : (d + 1) * home]

    p_copies = []
    for o in (2, 1, 3):
        to = lax.rem(me + o, insts)
        copy = pltpu.make_async_remote_copy(
            src_ref=p_send.at[to],
            dst_ref=p_recv.at[o - 1],
            send_sem=p_ssem.at[o - 1],
            recv_sem=p_rsem.at[o - 1],
            device_id={"inst": to},
            device_id_type=MESH,
        )
        copy.start()
        p_copies.append(copy)
    for copy in p_copies:
        copy.wait_recv()

    stats = [p_send[me, heads * home :, :]]
    stats += [p_recv[o, heads * home :, :] for o in range(insts - 1)]
    highest = own
    for s in stats:
        highest = jnp.maximum(highest, s)
    own_factor = jnp.exp(own - highest)
    total = own_factor
    factors = []
    for s in stats:
        f = jnp.exp(s - highest)
        total = total + f * pltpu.roll(s, 128 - heads, 1)
        factors.append(f)
    inverse = 1.0 / total
    own_factor = own_factor * inverse
    factors = [f * inverse for f in factors]
    merged = []
    for h in range(heads):
        at = slice(h * home, (h + 1) * home)
        acc = own_factor[:, h : h + 1] * own_v
        acc = acc + factors[0][:, h : h + 1] * p_send[me, at, :]
        for o in range(insts - 1):
            acc = acc + factors[o + 1][:, h : h + 1] * p_recv[o, at, :]
        merged.append(acc)

    lower = iota((8, 128), 0) < part
    for u in range(home // 8):
        first, second = [], []
        for h in range(0, heads, 2):
            a = merged[h][u * 8 : (u + 1) * 8]
            b = merged[h + 1][u * 8 : (u + 1) * 8]
            first.append(jnp.where(lower, a, pltpu.roll(b, part, 0)))
            second.append(jnp.where(lower, pltpu.roll(a, part, 0), b))
        r_send[2 * u] = jnp.concatenate(first, axis=0).astype(BF16)
        r_send[2 * u + 1] = jnp.concatenate(second, axis=0).astype(BF16)
    r_copies = []
    for t in range(tps):
        copy = pltpu.make_async_remote_copy(
            src_ref=r_send.at[t],
            dst_ref=out_ref.at[tp],
            send_sem=r_ssem.at[t],
            recv_sem=r_rsem.at[tp],
            device_id={"section": after, "tp": t},
            device_id_type=MESH,
        )
        copy.start()
        r_copies.append(copy)
    for t in range(tps):
        pltpu.make_async_remote_copy(
            src_ref=r_send.at[t],
            dst_ref=out_ref.at[t],
            send_sem=r_ssem.at[t],
            recv_sem=r_rsem.at[t],
            device_id={"section": after, "tp": t},
            device_id_type=MESH,
        ).wait_recv()
    for copy in q_copies + p_copies + r_copies:
        copy.wait_send()


def shards(queries, new_kv, kv_pages, lengths, block_tables):
    sections = lax.axis_size("section")
    insts = lax.axis_size("inst")
    tps = lax.axis_size("tp")
    home = queries.shape[1]
    heads = queries.shape[2] // HEAD_DIM
    pool, page = kv_pages.shape[1], kv_pages.shape[3]
    rows, slots = block_tables.shape[1:]
    part = home // tps
    sizes = (sections, insts, tps, home, pool, slots, page, heads)
    message = (heads + 1) * home
    out = pl.pallas_call(
        functools.partial(kernel, sizes),
        out_shape=jax.ShapeDtypeStruct((tps, heads * part, HEAD_DIM), BF16),
        in_specs=[pl.BlockSpec(memory_space=pl.ANY)] * 5,
        out_specs=pl.BlockSpec(memory_space=pl.ANY),
        scratch_shapes=[
            pltpu.VMEM((rows, heads * HEAD_DIM), BF16),
            pltpu.VMEM((2 * home, HEAD_DIM), BF16),
            pltpu.VMEM((2 * home, HEAD_DIM), F32),
            pltpu.VMEM((pool, 2, page, HEAD_DIM), BF16),
            pltpu.VMEM((1, rows), jnp.int32),
            pltpu.VMEM((slots, 1, rows), jnp.int32),
            pltpu.VMEM((heads, pool, HEAD_DIM), F32),
            pltpu.VMEM((heads, pool, HEAD_DIM), F32),
            pltpu.VMEM((heads, pool, HEAD_DIM), F32),
            pltpu.VMEM((insts, message, HEAD_DIM), F32),
            pltpu.VMEM((insts - 1, message, HEAD_DIM), F32),
            pltpu.VMEM((tps, heads * part, HEAD_DIM), BF16),
            pltpu.SemaphoreType.DMA((4,)),
            pltpu.SemaphoreType.DMA((4,)),
            pltpu.SemaphoreType.DMA((insts - 1,)),
            pltpu.SemaphoreType.DMA((insts - 1,)),
            pltpu.SemaphoreType.DMA((insts - 1,)),
            pltpu.SemaphoreType.DMA((insts - 1,)),
            pltpu.SemaphoreType.DMA((tps,)),
            pltpu.SemaphoreType.DMA((tps,)),
        ],
        compiler_params=pltpu.CompilerParams(
            collective_id=0, has_side_effects=True, vmem_limit_bytes=32 * 1024 * 1024
        ),
    )(
        queries[0],
        new_kv[0].reshape(2 * home, HEAD_DIM),
        kv_pages[0],
        lengths,
        block_tables[0].T.reshape(slots, 1, rows),
    )
    out = out.reshape(tps, heads, part, HEAD_DIM).transpose(2, 0, 1, 3)
    return out.reshape(1, part, tps * heads * HEAD_DIM)


def solution(mesh):
    placed = (
        P("section", "inst", "tp"),
        P("section", "inst", None, "tp"),
        P("section", "inst", None, None, "tp"),
        P("section", None),
        P("section", None, None),
    )
    return jax.shard_map(
        shards,
        mesh=mesh,
        in_specs=placed,
        out_specs=P("section", ("inst", "tp"), None),
        check_vma=False,
    )
```

```python
import functools
import math

import jax
import jax.numpy as jnp
from jax import lax
from jax.experimental import pallas as pl
from jax.experimental.pallas import tpu as pltpu
from jax.sharding import PartitionSpec as P

HEAD_DIM = 128
NEGATIVE = -1e30
GROUP = 8
CHUNKS = 2
ORDER = (2, 1, 3)
LEVELS = 32767.0
TINY = 1e-30
MESH = pl.DeviceIdType.MESH
F32 = jnp.float32
BF16 = jnp.bfloat16


def iota(shape, dim):
    return lax.broadcasted_iota(jnp.int32, shape, dim)


def dot(a, b):
    return lax.dot_general(a, b, (((1,), (0,)), ((), ())), preferred_element_type=F32)


def dot_nt(a, b):
    return lax.dot_general(a, b, (((1,), (1,)), ((), ())), preferred_element_type=F32)


def split(x):
    high = x.astype(BF16)
    return high, (x - high.astype(F32)).astype(BF16)


def kernel(
    sizes,
    q_hbm,
    fresh_hbm,
    kv_hbm,
    len_hbm,
    table_hbm,
    out_ref,
    q_all,
    fresh,
    fresh_f,
    kv,
    length,
    table,
    score_buf,
    weight_buf,
    page_x,
    page_m,
    page_s,
    p_send,
    p_recv,
    s_send,
    s_recv,
    r_send,
    load_sem,
    kv_sem,
    q_ssem,
    q_rsem,
    p_ssem,
    p_rsem,
    s_ssem,
    s_rsem,
    r_ssem,
    r_rsem,
):
    sections, insts, tps, home, pool, slots, page, heads = sizes
    rows = home * insts
    part = home // tps
    scale = 1.0 / math.sqrt(HEAD_DIM)
    sec = lax.axis_index("section")
    me = lax.axis_index("inst")
    tp = lax.axis_index("tp")
    before = lax.rem(sec + sections - 1, sections)
    after = lax.rem(sec + 1, sections)
    my_rows = pl.ds(pl.multiple_of(me * home, home), home)

    barrier = pltpu.get_barrier_semaphore()
    for o in range(1, insts):
        pl.semaphore_signal(
            barrier, inc=1, device_id={"inst": lax.rem(me + o, insts)}, device_id_type=MESH
        )
    for t in range(tps):
        pl.semaphore_signal(
            barrier, inc=1, device_id={"section": before, "tp": t}, device_id_type=MESH
        )
    load_q = pltpu.make_async_copy(q_hbm, q_all.at[my_rows], load_sem.at[0])
    load_fresh = pltpu.make_async_copy(fresh_hbm, fresh, load_sem.at[1])
    load_len = pltpu.make_async_copy(len_hbm, length, load_sem.at[2])
    load_table = pltpu.make_async_copy(table_hbm, table, load_sem.at[3])
    load_table.start()
    load_len.start()
    pl.semaphore_wait(barrier, insts - 1 + tps)

    q_copies = []
    for o in ORDER:
        copy = pltpu.make_async_remote_copy(
            src_ref=q_hbm,
            dst_ref=q_all.at[my_rows],
            send_sem=q_ssem.at[o - 1],
            recv_sem=q_rsem.at[o - 1],
            device_id={"inst": lax.rem(me + o, insts)},
            device_id_type=MESH,
        )
        copy.start()
        q_copies.append(copy)
    load_q.start()
    load_fresh.start()
    chunks = kv_sem.shape[0]
    per = pool // chunks
    load_kv = [
        pltpu.make_async_copy(
            kv_hbm.at[pl.ds(c * per, per)], kv.at[pl.ds(c * per, per)], kv_sem.at[c]
        )
        for c in range(chunks)
    ]
    for copy in load_kv:
        copy.start()

    load_len.wait()
    load_table.wait()
    page_id = iota((pool, rows), 0)
    counted = jnp.zeros((pool, rows), jnp.int32)
    for k in range(slots):
        local = table[k] - me * pool
        live = jnp.clip(length[...] - k * page, 0, page)
        counted = counted + jnp.where(page_id == local, live, 0)
    owned = counted > 0
    owner_f = jnp.where(owned, 1.0, 0.0).astype(F32)
    owner = owner_f.astype(BF16)
    owner_t = owner_f.T.astype(BF16)
    owner_t2 = jnp.concatenate([owner_t, owner_t], axis=1)
    tokens = dot(counted.astype(F32).astype(BF16), jnp.ones((rows, 128), BF16))

    load_fresh.wait()
    load_q.wait()
    fresh_f[...] = fresh[...].astype(F32)
    own_k = fresh_f[pl.ds(0, home, stride=2), :]
    own_v = fresh_f[pl.ds(1, home, stride=2), :]
    lane = iota((home, 128), 1)
    own = jnp.zeros((home, 128), F32)
    q_mine = q_all[my_rows, :].astype(F32)
    for h in range(heads):
        score = jnp.sum(q_mine[:, h * 128 : (h + 1) * 128] * own_k, axis=1, keepdims=True) * scale
        own = jnp.where(lane == h, score, own)

    for copy in load_kv:
        copy.wait()
    for copy in q_copies:
        copy.wait_recv()
    picked = dot(owner, q_all[...])

    stack = heads * GROUP
    groups = pool // GROUP
    row_page = lax.rem(iota((stack, 128), 0), GROUP)
    per_tile = 128 // page
    tiles = GROUP // per_tile
    tile_of = row_page // per_tile
    token = iota((stack, 128), 1) - lax.rem(row_page, per_tile) * page
    token_f = token.astype(F32)
    for g in range(groups):
        at = slice(g * GROUP, (g + 1) * GROUP)
        group_q = jnp.concatenate(
            [picked[at, h * 128 : (h + 1) * 128] for h in range(heads)], axis=0
        ).astype(BF16)
        full = dot_nt(group_q, kv[at, 0].reshape(GROUP * page, 128))
        scores = full[:, :128]
        for c in range(1, tiles):
            scores = jnp.where(tile_of == c, full[:, c * 128 : (c + 1) * 128], scores)
        score_buf[g] = scores
    for g in range(groups):
        at = slice(g * GROUP, (g + 1) * GROUP)
        limit = jnp.concatenate([tokens[at]] * heads, axis=0)
        valid = (token >= 0) & (token_f < limit)
        scores = jnp.where(valid, score_buf[g] * scale, NEGATIVE)
        highest = jnp.max(scores, axis=1, keepdims=True)
        weights = jnp.where(valid, jnp.exp(scores - highest), 0.0)
        total = jnp.sum(weights, axis=1, keepdims=True)
        weight_buf[g] = weights
        page_m[:, at, :] = jnp.broadcast_to(highest, (stack, 128)).reshape(heads, GROUP, 128)
        page_s[:, at, :] = jnp.broadcast_to(total, (stack, 128)).reshape(heads, GROUP, 128)
    for g in range(groups):
        at = slice(g * GROUP, (g + 1) * GROUP)
        weights = weight_buf[g]
        spread = jnp.concatenate(
            [jnp.where(tile_of == c, weights, 0.0).astype(BF16) for c in range(tiles)], axis=1
        )
        x = dot(spread, kv[at, 1].reshape(GROUP * page, 128))
        page_x[:, at, :] = x.reshape(heads, GROUP, 128)

    refs = []
    for h in range(heads):
        rounded = page_m[h].astype(BF16).astype(F32)
        refs.append(jnp.max(jnp.where(owned, rounded, NEGATIVE), axis=0, keepdims=True))
    ref_t = jnp.concatenate(refs + [jnp.zeros((128 - heads, rows), F32)], axis=0).T
    pool_lane = iota((pool, 128), 1)
    row_lane = iota((rows, 128), 1)
    span = heads // CHUNKS
    wide = span * home
    p_copies, s_copies = [], []
    for c in range(CHUNKS):
        chunk = range(c * span, (c + 1) * span)
        sums = jnp.zeros((pool, 128), F32)
        stat = jnp.where(row_lane < heads, ref_t, 0.0)
        for h in chunk[::2]:
            sides = []
            for j in (h, h + 1):
                page_ref = dot_nt(owner, jnp.broadcast_to(refs[j], (128, rows)).astype(BF16))
                factor = jnp.exp(page_m[j] - page_ref)
                sums = jnp.where(pool_lane == heads + j, factor * page_s[j], sums)
                high, low = split(factor * page_x[j])
                sides.append(jnp.concatenate([high, low], axis=0))
            both = dot(owner_t2, jnp.concatenate(sides, axis=1))
            for j in range(2):
                x = both[:, j * 128 : (j + 1) * 128]
                largest = jnp.maximum(jnp.max(jnp.abs(x), axis=1, keepdims=True), TINY)
                code = jnp.round(x * (LEVELS / largest)).astype(jnp.int32).astype(jnp.int16)
                stat = jnp.where(row_lane == 2 * heads + h + j, largest * (1.0 / LEVELS), stat)
                first = (h + j - c * span) * home
                for d in range(insts):
                    p_send[d, c, first : first + home, :] = code[d * home : (d + 1) * home]
        high, low = split(sums)
        stat = stat + dot(owner_t2, jnp.concatenate([high, low], axis=0))
        for d in range(insts):
            s_send[d, c] = stat[d * home : (d + 1) * home]
        for o in ORDER:
            to = lax.rem(me + o, insts)
            for copies, src, dst, ssem, rsem in (
                (s_copies, s_send, s_recv, s_ssem, s_rsem),
                (p_copies, p_send, p_recv, p_ssem, p_rsem),
            ):
                copy = pltpu.make_async_remote_copy(
                    src_ref=src.at[to, c],
                    dst_ref=dst.at[o - 1, c],
                    send_sem=ssem.at[c, o - 1],
                    recv_sem=rsem.at[c, o - 1],
                    device_id={"inst": to},
                    device_id_type=MESH,
                )
                copy.start()
                copies.append(copy)

    lower = iota((8, 128), 0) < part
    r_copies = []
    half = span * part
    others = insts - 1
    for c in range(CHUNKS):
        for copy in s_copies[c * others : (c + 1) * others]:
            copy.wait_recv()
        stats = [s_send[me, c]] + [s_recv[o, c] for o in range(others)]
        highest = own
        for s in stats:
            highest = jnp.maximum(highest, s)
        own_factor = jnp.exp(own - highest)
        total = own_factor
        factors = []
        for s in stats:
            f = jnp.exp(s - highest)
            total = total + f * pltpu.roll(s, 128 - heads, 1)
            factors.append(f * pltpu.roll(s, 128 - 2 * heads, 1))
        inverse = 1.0 / total
        own_factor = own_factor * inverse
        factors = [f * inverse for f in factors]
        for copy in p_copies[c * others : (c + 1) * others]:
            copy.wait_recv()
        merged = []
        for h in range(c * span, (c + 1) * span):
            at = slice((h - c * span) * home, (h + 1 - c * span) * home)
            acc = own_factor[:, h : h + 1] * own_v
            acc = acc + factors[0][:, h : h + 1] * p_send[me, c, at, :].astype(F32)
            for o in range(others):
                acc = acc + factors[o + 1][:, h : h + 1] * p_recv[o, c, at, :].astype(F32)
            merged.append(acc)
        for u in range(home // 8):
            first, second = [], []
            for h in range(0, span, 2):
                a = merged[h][u * 8 : (u + 1) * 8]
                b = merged[h + 1][u * 8 : (u + 1) * 8]
                first.append(jnp.where(lower, a, pltpu.roll(b, part, 0)))
                second.append(jnp.where(lower, pltpu.roll(a, part, 0), b))
            r_send[2 * u, c] = jnp.concatenate(first, axis=0).astype(BF16)
            r_send[2 * u + 1, c] = jnp.concatenate(second, axis=0).astype(BF16)
        for t in range(tps):
            copy = pltpu.make_async_remote_copy(
                src_ref=r_send.at[t, c],
                dst_ref=out_ref.at[tp, pl.ds(c * half, half)],
                send_sem=r_ssem.at[c, t],
                recv_sem=r_rsem.at[c, tp],
                device_id={"section": after, "tp": t},
                device_id_type=MESH,
            )
            copy.start()
            r_copies.append(copy)
    for c in range(CHUNKS):
        for t in range(tps):
            pltpu.make_async_remote_copy(
                src_ref=r_send.at[t, c],
                dst_ref=out_ref.at[t, pl.ds(c * half, half)],
                send_sem=r_ssem.at[c, t],
                recv_sem=r_rsem.at[c, t],
                device_id={"section": after, "tp": t},
                device_id_type=MESH,
            ).wait_recv()
    for copy in q_copies + s_copies + p_copies + r_copies:
        copy.wait_send()


def shards(queries, new_kv, kv_pages, lengths, block_tables):
    sections = lax.axis_size("section")
    insts = lax.axis_size("inst")
    tps = lax.axis_size("tp")
    home = queries.shape[1]
    heads = queries.shape[2] // HEAD_DIM
    pool, page = kv_pages.shape[1], kv_pages.shape[3]
    rows, slots = block_tables.shape[1:]
    part = home // tps
    sizes = (sections, insts, tps, home, pool, slots, page, heads)
    others = insts - 1
    groups, stack, wide = pool // GROUP, heads * GROUP, heads // CHUNKS * home
    out = pl.pallas_call(
        functools.partial(kernel, sizes),
        out_shape=pltpu.VMEM((tps, heads * part, HEAD_DIM), BF16),
        in_specs=[pl.BlockSpec(memory_space=pltpu.HBM)] * 5,
        out_specs=pl.BlockSpec(memory_space=pltpu.VMEM),
        scratch_shapes=[
            pltpu.VMEM((rows, heads * HEAD_DIM), BF16),
            pltpu.VMEM((2 * home, HEAD_DIM), BF16),
            pltpu.VMEM((2 * home, HEAD_DIM), F32),
            pltpu.VMEM((pool, 2, page, HEAD_DIM), BF16),
            pltpu.VMEM((1, rows), jnp.int32),
            pltpu.VMEM((slots, 1, rows), jnp.int32),
            pltpu.VMEM((groups, stack, 128), F32),
            pltpu.VMEM((groups, stack, 128), F32),
            pltpu.VMEM((heads, pool, HEAD_DIM), F32),
            pltpu.VMEM((heads, pool, HEAD_DIM), F32),
            pltpu.VMEM((heads, pool, HEAD_DIM), F32),
            pltpu.VMEM((insts, CHUNKS, wide, HEAD_DIM), jnp.int16),
            pltpu.VMEM((others, CHUNKS, wide, HEAD_DIM), jnp.int16),
            pltpu.VMEM((insts, CHUNKS, home, 128), F32),
            pltpu.VMEM((others, CHUNKS, home, 128), F32),
            pltpu.VMEM((tps, CHUNKS, heads // CHUNKS * part, HEAD_DIM), BF16),
            pltpu.SemaphoreType.DMA((4,)),
            pltpu.SemaphoreType.DMA((4,)),
            pltpu.SemaphoreType.DMA((others,)),
            pltpu.SemaphoreType.DMA((others,)),
            pltpu.SemaphoreType.DMA((CHUNKS, others)),
            pltpu.SemaphoreType.DMA((CHUNKS, others)),
            pltpu.SemaphoreType.DMA((CHUNKS, others)),
            pltpu.SemaphoreType.DMA((CHUNKS, others)),
            pltpu.SemaphoreType.DMA((CHUNKS, tps)),
            pltpu.SemaphoreType.DMA((CHUNKS, tps)),
        ],
        compiler_params=pltpu.CompilerParams(
            collective_id=0, has_side_effects=True, vmem_limit_bytes=32 * 1024 * 1024
        ),
    )(
        *(
            pltpu.with_memory_space_constraint(x, pltpu.HBM)
            for x in (
                queries[0],
                new_kv[0].reshape(2 * home, HEAD_DIM),
                kv_pages[0],
                lengths,
                jnp.transpose(block_tables, (2, 0, 1)),
            )
        )
    )
    out = out.reshape(tps, heads, part, HEAD_DIM).transpose(2, 0, 1, 3)
    return out.reshape(1, part, tps * heads * HEAD_DIM)


def solution(mesh):
    placed = (
        P("section", "inst", "tp"),
        P("section", "inst", None, "tp"),
        P("section", "inst", None, None, "tp"),
        P("section", None),
        P("section", None, None),
    )
    return jax.shard_map(
        shards,
        mesh=mesh,
        in_specs=placed,
        out_specs=P("section", ("inst", "tp"), None),
        check_vma=False,
    )
```

```python
import functools
import math

import jax
import jax.numpy as jnp
from jax import lax
from jax.experimental import pallas as pl
from jax.experimental.pallas import tpu as pltpu
from jax.sharding import PartitionSpec as P

HEAD_DIM = 128
NEGATIVE = -1e30
GROUP = 8
CHUNKS = 2
ORDER = (1, 3, 2)
LEVELS = 32767.0
TINY = 1e-30
MESH = pl.DeviceIdType.MESH
F32 = jnp.float32
BF16 = jnp.bfloat16


def iota(shape, dim):
    return lax.broadcasted_iota(jnp.int32, shape, dim)


def dot(a, b):
    return lax.dot_general(a, b, (((1,), (0,)), ((), ())), preferred_element_type=F32)


def dot_nt(a, b):
    return lax.dot_general(a, b, (((1,), (1,)), ((), ())), preferred_element_type=F32)


def split(x):
    high = x.astype(BF16)
    return high, (x - high.astype(F32)).astype(BF16)


def arrived(ref, sem):
    pltpu.make_async_copy(ref, ref, sem).wait()


def kernel(
    sizes,
    q_hbm,
    fresh_hbm,
    kv_hbm,
    len_hbm,
    table_hbm,
    out_ref,
    q_all,
    fresh,
    fresh_f,
    kv,
    length,
    table,
    score_buf,
    weight_buf,
    page_x,
    page_m,
    page_s,
    p_send,
    p_recv,
    s_send,
    s_recv,
    r_send,
    load_sem,
    kv_sem,
    q_ssem,
    q_rsem,
    p_ssem,
    p_rsem,
    s_ssem,
    s_rsem,
    r_ssem,
    r_rsem,
):
    sections, insts, tps, home, pool, slots, page, heads = sizes
    rows = home * insts
    part = home // tps
    scale = 1.0 / math.sqrt(HEAD_DIM)
    sec = lax.axis_index("section")
    me = lax.axis_index("inst")
    tp = lax.axis_index("tp")
    before = lax.rem(sec + sections - 1, sections)
    after = lax.rem(sec + 1, sections)
    my_rows = pl.ds(pl.multiple_of(me * home, home), home)

    span = heads // CHUNKS
    width = span * HEAD_DIM
    load_q = [
        pltpu.make_async_copy(
            q_hbm.at[:, pl.ds(c * width, width)], q_all.at[c, my_rows], load_sem.at[c]
        )
        for c in range(CHUNKS)
    ]
    for copy in load_q:
        copy.start()

    barrier = pltpu.get_barrier_semaphore()
    for o in range(1, insts):
        pl.semaphore_signal(
            barrier, inc=1, device_id={"inst": lax.rem(me + o, insts)}, device_id_type=MESH
        )
    for t in range(tps):
        pl.semaphore_signal(
            barrier, inc=1, device_id={"section": before, "tp": t}, device_id_type=MESH
        )
    load_fresh = pltpu.make_async_copy(fresh_hbm, fresh, load_sem.at[CHUNKS])
    load_len = pltpu.make_async_copy(len_hbm, length, load_sem.at[CHUNKS + 1])
    load_table = pltpu.make_async_copy(table_hbm, table, load_sem.at[CHUNKS + 2])
    parts = kv_sem.shape[0]
    per = pool // parts
    load_kv = [
        pltpu.make_async_copy(
            kv_hbm.at[pl.ds(c * per, per)], kv.at[pl.ds(c * per, per)], kv_sem.at[c]
        )
        for c in range(parts)
    ]
    for copy in [load_table, load_len, load_fresh] + load_kv:
        copy.start()
    pl.semaphore_wait(barrier, insts - 1 + tps)

    for c in range(CHUNKS):
        load_q[c].wait()
        for o in ORDER:
            copy = pltpu.make_async_remote_copy(
                src_ref=q_all.at[c, my_rows],
                dst_ref=q_all.at[c, my_rows],
                send_sem=q_ssem.at[c],
                recv_sem=q_rsem.at[c],
                device_id={"inst": lax.rem(me + o, insts)},
                device_id_type=MESH,
            )
            copy.start()

    load_len.wait()
    load_table.wait()
    page_id = iota((pool, rows), 0)
    counted = jnp.zeros((pool, rows), jnp.int32)
    for k in range(slots):
        local = table[k] - me * pool
        live = jnp.clip(length[...] - k * page, 0, page)
        counted = counted + jnp.where(page_id == local, live, 0)
    owned = counted > 0
    owner_f = jnp.where(owned, 1.0, 0.0).astype(F32)
    owner = owner_f.astype(BF16)
    owner_t = owner_f.T.astype(BF16)
    owner_t2 = jnp.concatenate([owner_t, owner_t], axis=1)
    tokens = dot(counted.astype(F32).astype(BF16), jnp.ones((rows, 128), BF16))

    load_fresh.wait()
    fresh_f[...] = fresh[...].astype(F32)
    own_k = fresh_f[pl.ds(0, home, stride=2), :]
    own_v = fresh_f[pl.ds(1, home, stride=2), :]
    lane = iota((home, 128), 1)
    own = jnp.zeros((home, 128), F32)
    for c in range(CHUNKS):
        q_mine = q_all[c, my_rows, :].astype(F32)
        for h in range(span):
            score = jnp.sum(q_mine[:, h * 128 : (h + 1) * 128] * own_k, axis=1, keepdims=True)
            own = jnp.where(lane == c * span + h, score * scale, own)

    for copy in load_kv:
        copy.wait()

    others = insts - 1
    stack = span * GROUP
    groups = pool // GROUP
    row_page = lax.rem(iota((stack, 128), 0), GROUP)
    per_tile = 128 // page
    tiles = GROUP // per_tile
    tile_of = row_page // per_tile
    token = iota((stack, 128), 1) - lax.rem(row_page, per_tile) * page
    token_f = token.astype(F32)
    pool_lane = iota((pool, 128), 1)
    row_lane = iota((rows, 128), 1)
    for c in range(CHUNKS):
        arrived(q_all.at[c, pl.ds(0, others * home)], q_rsem.at[c])
        picked = dot(owner, q_all[c])
        for g in range(groups):
            at = slice(g * GROUP, (g + 1) * GROUP)
            group_q = jnp.concatenate(
                [picked[at, h * 128 : (h + 1) * 128] for h in range(span)], axis=0
            ).astype(BF16)
            full = dot_nt(group_q, kv[at, 0].reshape(GROUP * page, 128))
            scores = full[:, :128]
            for i in range(1, tiles):
                scores = jnp.where(tile_of == i, full[:, i * 128 : (i + 1) * 128], scores)
            score_buf[c, g] = scores
        for g in range(groups):
            at = slice(g * GROUP, (g + 1) * GROUP)
            limit = jnp.concatenate([tokens[at]] * span, axis=0)
            valid = (token >= 0) & (token_f < limit)
            scores = jnp.where(valid, score_buf[c, g] * scale, NEGATIVE)
            highest = jnp.max(scores, axis=1, keepdims=True)
            weights = jnp.where(valid, jnp.exp(scores - highest), 0.0)
            total = jnp.sum(weights, axis=1, keepdims=True)
            weight_buf[c, g] = weights
            page_m[c, :, at, :] = jnp.broadcast_to(highest, (stack, 128)).reshape(span, GROUP, 128)
            page_s[c, :, at, :] = jnp.broadcast_to(total, (stack, 128)).reshape(span, GROUP, 128)
        for g in range(groups):
            at = slice(g * GROUP, (g + 1) * GROUP)
            weights = weight_buf[c, g]
            spread = jnp.concatenate(
                [jnp.where(tile_of == i, weights, 0.0).astype(BF16) for i in range(tiles)], axis=1
            )
            x = dot(spread, kv[at, 1].reshape(GROUP * page, 128))
            page_x[c, :, at, :] = x.reshape(span, GROUP, 128)

        refs = []
        for h in range(span):
            rounded = page_m[c, h].astype(BF16).astype(F32)
            refs.append(jnp.max(jnp.where(owned, rounded, NEGATIVE), axis=0, keepdims=True))
        sums = jnp.zeros((pool, 128), F32)
        stat = jnp.concatenate(refs + [jnp.zeros((128 - span, rows), F32)], axis=0).T
        for h in range(0, span, 2):
            sides = []
            for j in (h, h + 1):
                page_ref = dot_nt(owner, jnp.broadcast_to(refs[j], (128, rows)).astype(BF16))
                factor = jnp.exp(page_m[c, j] - page_ref)
                sums = jnp.where(pool_lane == span + j, factor * page_s[c, j], sums)
                high, low = split(factor * page_x[c, j])
                sides.append(jnp.concatenate([high, low], axis=0))
            both = dot(owner_t2, jnp.concatenate(sides, axis=1))
            for j in range(2):
                x = both[:, j * 128 : (j + 1) * 128]
                largest = jnp.maximum(jnp.max(jnp.abs(x), axis=1, keepdims=True), TINY)
                code = jnp.round(x * (LEVELS / largest)).astype(jnp.int32).astype(jnp.int16)
                stat = jnp.where(row_lane == 2 * span + h + j, largest * (1.0 / LEVELS), stat)
                first = (h + j) * home
                for d in range(insts):
                    p_send[d, c, first : first + home, :] = code[d * home : (d + 1) * home]
        high, low = split(sums)
        stat = stat + dot(owner_t2, jnp.concatenate([high, low], axis=0))
        for d in range(insts):
            s_send[d, c] = stat[d * home : (d + 1) * home]
        for o in ORDER:
            to = lax.rem(me + o, insts)
            for src, dst, ssem, rsem in (
                (s_send, s_recv, s_ssem, s_rsem),
                (p_send, p_recv, p_ssem, p_rsem),
            ):
                copy = pltpu.make_async_remote_copy(
                    src_ref=src.at[to, c],
                    dst_ref=dst.at[c, o - 1],
                    send_sem=ssem.at[c],
                    recv_sem=rsem.at[c],
                    device_id={"inst": to},
                    device_id_type=MESH,
                )
                copy.start()

    lower = iota((8, 128), 0) < part
    half = span * part
    for c in range(CHUNKS):
        arrived(s_recv.at[c], s_rsem.at[c])
        stats = [s_send[me, c]] + [s_recv[c, o] for o in range(others)]
        mine = pltpu.roll(own, 128 - c * span, 1) if c else own
        highest = mine
        for s in stats:
            highest = jnp.maximum(highest, s)
        own_factor = jnp.exp(mine - highest)
        total = own_factor
        factors = []
        for s in stats:
            f = jnp.exp(s - highest)
            total = total + f * pltpu.roll(s, 128 - span, 1)
            factors.append(f * pltpu.roll(s, 128 - 2 * span, 1))
        inverse = 1.0 / total
        own_factor = own_factor * inverse
        factors = [f * inverse for f in factors]
        arrived(p_recv.at[c], p_rsem.at[c])
        merged = []
        for h in range(span):
            at = slice(h * home, (h + 1) * home)
            acc = own_factor[:, h : h + 1] * own_v
            acc = acc + factors[0][:, h : h + 1] * p_send[me, c, at, :].astype(F32)
            for o in range(others):
                acc = acc + factors[o + 1][:, h : h + 1] * p_recv[c, o, at, :].astype(F32)
            merged.append(acc)
        for u in range(home // 8):
            first, second = [], []
            for h in range(0, span, 2):
                a = merged[h][u * 8 : (u + 1) * 8]
                b = merged[h + 1][u * 8 : (u + 1) * 8]
                first.append(jnp.where(lower, a, pltpu.roll(b, part, 0)))
                second.append(jnp.where(lower, pltpu.roll(a, part, 0), b))
            r_send[c, 2 * u] = jnp.concatenate(first, axis=0).astype(BF16)
            r_send[c, 2 * u + 1] = jnp.concatenate(second, axis=0).astype(BF16)
        for t in range(tps):
            copy = pltpu.make_async_remote_copy(
                src_ref=r_send.at[c, t],
                dst_ref=out_ref.at[tp, pl.ds(c * half, half)],
                send_sem=r_ssem.at[c],
                recv_sem=r_rsem.at[c],
                device_id={"section": after, "tp": t},
                device_id_type=MESH,
            )
            copy.start()
    for c in range(CHUNKS):
        arrived(q_all.at[c, pl.ds(0, others * home)], q_ssem.at[c])
        arrived(s_recv.at[c], s_ssem.at[c])
        arrived(p_recv.at[c], p_ssem.at[c])
        arrived(r_send.at[c], r_ssem.at[c])
    for c in range(CHUNKS):
        arrived(r_send.at[c], r_rsem.at[c])


def shards(queries, new_kv, kv_pages, lengths, block_tables):
    sections = lax.axis_size("section")
    insts = lax.axis_size("inst")
    tps = lax.axis_size("tp")
    home = queries.shape[1]
    heads = queries.shape[2] // HEAD_DIM
    pool, page = kv_pages.shape[1], kv_pages.shape[3]
    rows, slots = block_tables.shape[1:]
    part = home // tps
    sizes = (sections, insts, tps, home, pool, slots, page, heads)
    others = insts - 1
    span = heads // CHUNKS
    groups, stack, wide = pool // GROUP, span * GROUP, span * home
    out = pl.pallas_call(
        functools.partial(kernel, sizes),
        out_shape=pltpu.VMEM((tps, heads * part, HEAD_DIM), BF16),
        in_specs=[pl.BlockSpec(memory_space=pltpu.HBM)] * 5,
        out_specs=pl.BlockSpec(memory_space=pltpu.VMEM),
        scratch_shapes=[
            pltpu.VMEM((CHUNKS, rows, span * HEAD_DIM), BF16),
            pltpu.VMEM((2 * home, HEAD_DIM), BF16),
            pltpu.VMEM((2 * home, HEAD_DIM), F32),
            pltpu.VMEM((pool, 2, page, HEAD_DIM), BF16),
            pltpu.VMEM((1, rows), jnp.int32),
            pltpu.VMEM((slots, 1, rows), jnp.int32),
            pltpu.VMEM((CHUNKS, groups, stack, 128), F32),
            pltpu.VMEM((CHUNKS, groups, stack, 128), F32),
            pltpu.VMEM((CHUNKS, span, pool, HEAD_DIM), F32),
            pltpu.VMEM((CHUNKS, span, pool, HEAD_DIM), F32),
            pltpu.VMEM((CHUNKS, span, pool, HEAD_DIM), F32),
            pltpu.VMEM((insts, CHUNKS, wide, HEAD_DIM), jnp.int16),
            pltpu.VMEM((CHUNKS, others, wide, HEAD_DIM), jnp.int16),
            pltpu.VMEM((insts, CHUNKS, home, 128), F32),
            pltpu.VMEM((CHUNKS, others, home, 128), F32),
            pltpu.VMEM((CHUNKS, tps, span * part, HEAD_DIM), BF16),
            pltpu.SemaphoreType.DMA((CHUNKS + 3,)),
            pltpu.SemaphoreType.DMA((4,)),
            pltpu.SemaphoreType.DMA((CHUNKS,)),
            pltpu.SemaphoreType.DMA((CHUNKS,)),
            pltpu.SemaphoreType.DMA((CHUNKS,)),
            pltpu.SemaphoreType.DMA((CHUNKS,)),
            pltpu.SemaphoreType.DMA((CHUNKS,)),
            pltpu.SemaphoreType.DMA((CHUNKS,)),
            pltpu.SemaphoreType.DMA((CHUNKS,)),
            pltpu.SemaphoreType.DMA((CHUNKS,)),
        ],
        compiler_params=pltpu.CompilerParams(
            collective_id=0, has_side_effects=True, vmem_limit_bytes=32 * 1024 * 1024
        ),
    )(
        *(
            pltpu.with_memory_space_constraint(x, pltpu.HBM)
            for x in (
                queries[0],
                new_kv[0].reshape(2 * home, HEAD_DIM),
                kv_pages[0],
                lengths,
                jnp.transpose(block_tables, (2, 0, 1)),
            )
        )
    )
    out = out.reshape(tps, heads, part, HEAD_DIM).transpose(2, 0, 1, 3)
    return out.reshape(1, part, tps * heads * HEAD_DIM)


def solution(mesh):
    placed = (
        P("section", "inst", "tp"),
        P("section", "inst", None, "tp"),
        P("section", "inst", None, None, "tp"),
        P("section", None),
        P("section", None, None),
    )
    return jax.shard_map(
        shards,
        mesh=mesh,
        in_specs=placed,
        out_specs=P("section", ("inst", "tp"), None),
        check_vma=False,
    )
```

```python
import functools
import math

import jax
import jax.numpy as jnp
from jax import lax
from jax.experimental import pallas as pl
from jax.experimental.pallas import tpu as pltpu
from jax.sharding import PartitionSpec as P

HEAD_DIM = 128
NEGATIVE = -1e30
GROUP = 8
CHUNKS = 2
ORDER = (1, 3, 2)
LEVELS = 32767.0
TINY = 1e-30
MESH = pl.DeviceIdType.MESH
F32 = jnp.float32
BF16 = jnp.bfloat16


def iota(shape, dim):
    return lax.broadcasted_iota(jnp.int32, shape, dim)


def dot(a, b):
    return lax.dot_general(a, b, (((1,), (0,)), ((), ())), preferred_element_type=F32)


def dot_nt(a, b):
    return lax.dot_general(a, b, (((1,), (1,)), ((), ())), preferred_element_type=F32)


def split(x):
    high = x.astype(BF16)
    return high, (x - high.astype(F32)).astype(BF16)


def arrived(ref, sem):
    pltpu.make_async_copy(ref, ref, sem).wait()


def kernel(
    sizes,
    q_hbm,
    fresh_hbm,
    kv_hbm,
    len_hbm,
    table_hbm,
    out_ref,
    q_all,
    fresh,
    fresh_f,
    kv,
    keys,
    length,
    table,
    picked_buf,
    token_buf,
    score_buf,
    weight_buf,
    page_x,
    page_m,
    page_s,
    p_send,
    p_recv,
    s_send,
    s_recv,
    r_send,
    load_sem,
    kv_sem,
    q_ssem,
    q_rsem,
    p_ssem,
    p_rsem,
    s_ssem,
    s_rsem,
    r_ssem,
    r_rsem,
):
    sections, insts, tps, home, pool, slots, page, heads = sizes
    rows = home * insts
    part = home // tps
    scale = 1.0 / math.sqrt(HEAD_DIM)
    sec = lax.axis_index("section")
    me = lax.axis_index("inst")
    tp = lax.axis_index("tp")
    before = lax.rem(sec + sections - 1, sections)
    after = lax.rem(sec + 1, sections)
    my_rows = pl.ds(pl.multiple_of(me * home, home), home)

    span = heads // CHUNKS
    width = span * HEAD_DIM
    load_q = [
        pltpu.make_async_copy(
            q_hbm.at[:, pl.ds(c * width, width)], q_all.at[c, my_rows], load_sem.at[c]
        )
        for c in range(CHUNKS)
    ]
    for copy in load_q:
        copy.start()

    barrier = pltpu.get_barrier_semaphore()
    for o in range(1, insts):
        pl.semaphore_signal(
            barrier, inc=1, device_id={"inst": lax.rem(me + o, insts)}, device_id_type=MESH
        )
    for t in range(tps):
        pl.semaphore_signal(
            barrier, inc=1, device_id={"section": before, "tp": t}, device_id_type=MESH
        )
    load_fresh = pltpu.make_async_copy(fresh_hbm, fresh, load_sem.at[CHUNKS])
    load_len = pltpu.make_async_copy(len_hbm, length, load_sem.at[CHUNKS + 1])
    load_table = pltpu.make_async_copy(table_hbm, table, load_sem.at[CHUNKS + 2])
    parts = kv_sem.shape[0]
    per = pool // parts
    load_kv = [
        pltpu.make_async_copy(
            kv_hbm.at[pl.ds(c * per, per)], kv.at[pl.ds(c * per, per)], kv_sem.at[c]
        )
        for c in range(parts)
    ]
    for copy in [load_table, load_len, load_fresh] + load_kv:
        copy.start()
    pl.semaphore_wait(barrier, insts - 1 + tps)

    for c in range(CHUNKS):
        load_q[c].wait()
        for o in ORDER:
            copy = pltpu.make_async_remote_copy(
                src_ref=q_all.at[c, my_rows],
                dst_ref=q_all.at[c, my_rows],
                send_sem=q_ssem.at[c],
                recv_sem=q_rsem.at[c],
                device_id={"inst": lax.rem(me + o, insts)},
                device_id_type=MESH,
            )
            copy.start()

    load_len.wait()
    load_table.wait()
    page_id = iota((pool, rows), 0)
    counted = jnp.zeros((pool, rows), jnp.int32)
    for k in range(slots):
        local = table[k] - me * pool
        live = jnp.clip(length[...] - k * page, 0, page)
        counted = counted + jnp.where(page_id == local, live, 0)
    owned = counted > 0
    owner_f = jnp.where(owned, 1.0, 0.0).astype(F32)
    owner = owner_f.astype(BF16)
    owner_t = owner_f.T.astype(BF16)
    owner_t2 = jnp.concatenate([owner_t, owner_t], axis=1)
    token_buf[...] = dot(counted.astype(F32).astype(BF16), jnp.ones((rows, 128), BF16))

    load_fresh.wait()
    fresh_f[...] = fresh[...].astype(F32)
    own_k = fresh_f[pl.ds(0, home, stride=2), :]
    own_v = fresh_f[pl.ds(1, home, stride=2), :]
    lane = iota((home, 128), 1)
    own = jnp.zeros((home, 128), F32)
    for c in range(CHUNKS):
        q_mine = q_all[c, my_rows, :].astype(F32)
        for h in range(span):
            score = jnp.sum(q_mine[:, h * 128 : (h + 1) * 128] * own_k, axis=1, keepdims=True)
            own = jnp.where(lane == c * span + h, score * scale, own)

    for i in range(parts):
        load_kv[i].wait()
        for g in range(i * per // GROUP, (i + 1) * per // GROUP):
            at = slice(g * GROUP, (g + 1) * GROUP)
            keys[g] = kv[at, 0].reshape(GROUP * page, 128).T

    others = insts - 1
    stack = span * GROUP
    groups = pool // GROUP
    row_page = lax.rem(iota((stack, 128), 0), GROUP)
    per_tile = 128 // page
    tiles = GROUP // per_tile
    tile_of = row_page // per_tile
    token = iota((stack, 128), 1) - lax.rem(row_page, per_tile) * page
    token_f = token.astype(F32)
    pool_lane = iota((pool, 128), 1)
    row_lane = iota((rows, 128), 1)
    def wait_q(c):
        arrived(q_all.at[c, pl.ds(0, others * home)], q_rsem.at[c])

    def pick(c):
        picked_buf[c] = dot(owner, q_all[c])

    def score_group(c, g, carry):
        at = pl.ds(pl.multiple_of(g * GROUP, GROUP), GROUP)
        group_q = jnp.concatenate(
            [picked_buf[c, at, h * 128 : (h + 1) * 128] for h in range(span)], axis=0
        ).astype(BF16)
        full = dot(group_q, keys[g])
        scores = full[:, :128]
        for i in range(1, tiles):
            scores = jnp.where(tile_of == i, full[:, i * 128 : (i + 1) * 128], scores)
        score_buf[c, g] = scores
        return carry

    def weigh_group(c, g, carry):
        at = pl.ds(pl.multiple_of(g * GROUP, GROUP), GROUP)
        limit = jnp.concatenate([token_buf[at, :]] * span, axis=0)
        valid = (token >= 0) & (token_f < limit)
        scores = jnp.where(valid, score_buf[c, g] * scale, NEGATIVE)
        highest = jnp.max(scores, axis=1, keepdims=True)
        weights = jnp.where(valid, jnp.exp(scores - highest), 0.0)
        total = jnp.sum(weights, axis=1, keepdims=True)
        weight_buf[c, g] = weights
        page_m[c, :, at, :] = jnp.broadcast_to(highest, (stack, 128)).reshape(span, GROUP, 128)
        page_s[c, :, at, :] = jnp.broadcast_to(total, (stack, 128)).reshape(span, GROUP, 128)
        return carry

    def value_group(c, g, carry):
        at = pl.ds(pl.multiple_of(g * GROUP, GROUP), GROUP)
        weights = weight_buf[c, g]
        spread = jnp.concatenate(
            [jnp.where(tile_of == i, weights, 0.0).astype(BF16) for i in range(tiles)], axis=1
        )
        x = dot(spread, kv[at, 1].reshape(GROUP * page, 128))
        page_x[c, :, at, :] = x.reshape(span, GROUP, 128)
        return carry

    def groupwise(body, c):
        lax.fori_loop(0, groups, functools.partial(body, c), 0, unroll=groups)

    def combine(c):
        refs = []
        for h in range(span):
            rounded = page_m[c, h].astype(BF16).astype(F32)
            refs.append(jnp.max(jnp.where(owned, rounded, NEGATIVE), axis=0, keepdims=True))
        sums = jnp.zeros((pool, 128), F32)
        stat = jnp.concatenate(refs + [jnp.zeros((128 - span, rows), F32)], axis=0).T
        for h in range(0, span, 2):
            sides = []
            for j in (h, h + 1):
                page_ref = dot_nt(owner, jnp.broadcast_to(refs[j], (128, rows)).astype(BF16))
                factor = jnp.exp(page_m[c, j] - page_ref)
                sums = jnp.where(pool_lane == span + j, factor * page_s[c, j], sums)
                high, low = split(factor * page_x[c, j])
                sides.append(jnp.concatenate([high, low], axis=0))
            both = dot(owner_t2, jnp.concatenate(sides, axis=1))
            for j in range(2):
                x = both[:, j * 128 : (j + 1) * 128]
                largest = jnp.maximum(jnp.max(jnp.abs(x), axis=1, keepdims=True), TINY)
                code = jnp.round(x * (LEVELS / largest)).astype(jnp.int32).astype(jnp.int16)
                stat = jnp.where(row_lane == 2 * span + h + j, largest * (1.0 / LEVELS), stat)
                first = (h + j) * home
                for d in range(insts):
                    p_send[d, c, first : first + home, :] = code[d * home : (d + 1) * home]
        high, low = split(sums)
        stat = stat + dot(owner_t2, jnp.concatenate([high, low], axis=0))
        for d in range(insts):
            s_send[d, c] = stat[d * home : (d + 1) * home]

    def send(c):
        for o in ORDER:
            to = lax.rem(me + o, insts)
            for src, dst, ssem, rsem in (
                (s_send, s_recv, s_ssem, s_rsem),
                (p_send, p_recv, p_ssem, p_rsem),
            ):
                copy = pltpu.make_async_remote_copy(
                    src_ref=src.at[to, c],
                    dst_ref=dst.at[c, o - 1],
                    send_sem=ssem.at[c],
                    recv_sem=rsem.at[c],
                    device_id={"inst": to},
                    device_id_type=MESH,
                )
                copy.start()

    wait_q(0)
    pick(0)
    groupwise(score_group, 0)
    groupwise(weigh_group, 0)
    groupwise(value_group, 0)
    combine(0)
    send(0)
    wait_q(1)
    pick(1)
    groupwise(score_group, 1)
    groupwise(weigh_group, 1)
    groupwise(value_group, 1)
    combine(1)
    send(1)

    lower = iota((8, 128), 0) < part
    half = span * part
    for c in range(CHUNKS):
        arrived(s_recv.at[c], s_rsem.at[c])
        stats = [s_send[me, c]] + [s_recv[c, o] for o in range(others)]
        mine = pltpu.roll(own, 128 - c * span, 1) if c else own
        highest = mine
        for s in stats:
            highest = jnp.maximum(highest, s)
        own_factor = jnp.exp(mine - highest)
        total = own_factor
        factors = []
        for s in stats:
            f = jnp.exp(s - highest)
            total = total + f * pltpu.roll(s, 128 - span, 1)
            factors.append(f * pltpu.roll(s, 128 - 2 * span, 1))
        inverse = 1.0 / total
        own_factor = own_factor * inverse
        factors = [f * inverse for f in factors]
        arrived(p_recv.at[c], p_rsem.at[c])
        merged = []
        for h in range(span):
            at = slice(h * home, (h + 1) * home)
            acc = own_factor[:, h : h + 1] * own_v
            acc = acc + factors[0][:, h : h + 1] * p_send[me, c, at, :].astype(F32)
            for o in range(others):
                acc = acc + factors[o + 1][:, h : h + 1] * p_recv[c, o, at, :].astype(F32)
            merged.append(acc)
        for u in range(home // 8):
            first, second = [], []
            for h in range(0, span, 2):
                a = merged[h][u * 8 : (u + 1) * 8]
                b = merged[h + 1][u * 8 : (u + 1) * 8]
                first.append(jnp.where(lower, a, pltpu.roll(b, part, 0)))
                second.append(jnp.where(lower, pltpu.roll(a, part, 0), b))
            r_send[c, 2 * u] = jnp.concatenate(first, axis=0).astype(BF16)
            r_send[c, 2 * u + 1] = jnp.concatenate(second, axis=0).astype(BF16)
        for t in range(tps):
            copy = pltpu.make_async_remote_copy(
                src_ref=r_send.at[c, t],
                dst_ref=out_ref.at[tp, pl.ds(c * half, half)],
                send_sem=r_ssem.at[c],
                recv_sem=r_rsem.at[c],
                device_id={"section": after, "tp": t},
                device_id_type=MESH,
            )
            copy.start()
    for c in range(CHUNKS):
        arrived(q_all.at[c, pl.ds(0, others * home)], q_ssem.at[c])
        arrived(s_recv.at[c], s_ssem.at[c])
        arrived(p_recv.at[c], p_ssem.at[c])
        arrived(r_send.at[c], r_ssem.at[c])
    for c in range(CHUNKS):
        arrived(r_send.at[c], r_rsem.at[c])


def shards(queries, new_kv, kv_pages, lengths, block_tables):
    sections = lax.axis_size("section")
    insts = lax.axis_size("inst")
    tps = lax.axis_size("tp")
    home = queries.shape[1]
    heads = queries.shape[2] // HEAD_DIM
    pool, page = kv_pages.shape[1], kv_pages.shape[3]
    rows, slots = block_tables.shape[1:]
    part = home // tps
    sizes = (sections, insts, tps, home, pool, slots, page, heads)
    others = insts - 1
    span = heads // CHUNKS
    groups, stack, wide = pool // GROUP, span * GROUP, span * home
    out = pl.pallas_call(
        functools.partial(kernel, sizes),
        out_shape=pltpu.VMEM((tps, heads * part, HEAD_DIM), BF16),
        in_specs=[pl.BlockSpec(memory_space=pltpu.HBM)] * 5,
        out_specs=pl.BlockSpec(memory_space=pltpu.VMEM),
        scratch_shapes=[
            pltpu.VMEM((CHUNKS, rows, span * HEAD_DIM), BF16),
            pltpu.VMEM((2 * home, HEAD_DIM), BF16),
            pltpu.VMEM((2 * home, HEAD_DIM), F32),
            pltpu.VMEM((pool, 2, page, HEAD_DIM), BF16),
            pltpu.VMEM((groups, HEAD_DIM, GROUP * page), BF16),
            pltpu.VMEM((1, rows), jnp.int32),
            pltpu.VMEM((slots, 1, rows), jnp.int32),
            pltpu.VMEM((CHUNKS, pool, span * HEAD_DIM), F32),
            pltpu.VMEM((pool, 128), F32),
            pltpu.VMEM((CHUNKS, groups, stack, 128), F32),
            pltpu.VMEM((CHUNKS, groups, stack, 128), F32),
            pltpu.VMEM((CHUNKS, span, pool, HEAD_DIM), F32),
            pltpu.VMEM((CHUNKS, span, pool, HEAD_DIM), F32),
            pltpu.VMEM((CHUNKS, span, pool, HEAD_DIM), F32),
            pltpu.VMEM((insts, CHUNKS, wide, HEAD_DIM), jnp.int16),
            pltpu.VMEM((CHUNKS, others, wide, HEAD_DIM), jnp.int16),
            pltpu.VMEM((insts, CHUNKS, home, 128), F32),
            pltpu.VMEM((CHUNKS, others, home, 128), F32),
            pltpu.VMEM((CHUNKS, tps, span * part, HEAD_DIM), BF16),
            pltpu.SemaphoreType.DMA((CHUNKS + 3,)),
            pltpu.SemaphoreType.DMA((4,)),
            pltpu.SemaphoreType.DMA((CHUNKS,)),
            pltpu.SemaphoreType.DMA((CHUNKS,)),
            pltpu.SemaphoreType.DMA((CHUNKS,)),
            pltpu.SemaphoreType.DMA((CHUNKS,)),
            pltpu.SemaphoreType.DMA((CHUNKS,)),
            pltpu.SemaphoreType.DMA((CHUNKS,)),
            pltpu.SemaphoreType.DMA((CHUNKS,)),
            pltpu.SemaphoreType.DMA((CHUNKS,)),
        ],
        compiler_params=pltpu.CompilerParams(
            collective_id=0, has_side_effects=True, vmem_limit_bytes=32 * 1024 * 1024
        ),
    )(
        *(
            pltpu.with_memory_space_constraint(x, pltpu.HBM)
            for x in (
                queries[0],
                new_kv[0].reshape(2 * home, HEAD_DIM),
                kv_pages[0],
                lengths,
                jnp.transpose(block_tables, (2, 0, 1)),
            )
        )
    )
    out = out.reshape(tps, heads, part, HEAD_DIM).transpose(2, 0, 1, 3)
    return out.reshape(1, part, tps * heads * HEAD_DIM)


def solution(mesh):
    placed = (
        P("section", "inst", "tp"),
        P("section", "inst", None, "tp"),
        P("section", "inst", None, None, "tp"),
        P("section", None),
        P("section", None, None),
    )
    return jax.shard_map(
        shards,
        mesh=mesh,
        in_specs=placed,
        out_specs=P("section", ("inst", "tp"), None),
        check_vma=False,
    )
```

```python
import functools
import math

import jax
import jax.numpy as jnp
from jax import lax
from jax.experimental import pallas as pl
from jax.experimental.pallas import tpu as pltpu
from jax.sharding import PartitionSpec as P

HEAD_DIM = 128
NEGATIVE = -1e30
GROUP = 8
CHUNKS = 2
ORDER = (1, 3, 2)
LEVELS = 32767.0
TINY = 1e-30
MESH = pl.DeviceIdType.MESH
F32 = jnp.float32
BF16 = jnp.bfloat16


def iota(shape, dim):
    return lax.broadcasted_iota(jnp.int32, shape, dim)


def dot(a, b):
    return lax.dot_general(a, b, (((1,), (0,)), ((), ())), preferred_element_type=F32)


def dot_nt(a, b):
    return lax.dot_general(a, b, (((1,), (1,)), ((), ())), preferred_element_type=F32)


def split(x):
    high = x.astype(BF16)
    return high, (x - high.astype(F32)).astype(BF16)


def arrived(ref, sem):
    pltpu.make_async_copy(ref, ref, sem).wait()


def kernel(
    sizes,
    q_hbm,
    fresh_hbm,
    kv_hbm,
    len_hbm,
    table_hbm,
    out_ref,
    q_all,
    fresh,
    fresh_f,
    kv,
    keys,
    length,
    table,
    picked_buf,
    token_buf,
    score_buf,
    weight_buf,
    page_x,
    page_m,
    page_s,
    p_send,
    p_recv,
    s_send,
    s_recv,
    r_send,
    own_send,
    own_recv,
    load_sem,
    kv_sem,
    q_ssem,
    q_rsem,
    p_ssem,
    p_rsem,
    s_ssem,
    s_rsem,
    r_ssem,
    r_rsem,
    own_sem,
):
    sections, insts, tps, home, pool, slots, page, heads = sizes
    rows = home * insts
    part = home // tps
    scale = 1.0 / math.sqrt(HEAD_DIM)
    sec = lax.axis_index("section")
    me = lax.axis_index("inst")
    tp = lax.axis_index("tp")
    core = lax.rem(tp, 2)
    merger = tp + 1 - core
    merges = core == 1
    others = insts - 1
    before = lax.rem(sec + sections - 1, sections)
    after = lax.rem(sec + 1, sections)
    my_rows = pl.ds(pl.multiple_of(me * home, home), home)

    span = heads // CHUNKS
    width = span * HEAD_DIM
    load_q = [
        pltpu.make_async_copy(
            q_hbm.at[:, pl.ds(c * width, width)], q_all.at[c, my_rows], load_sem.at[c]
        )
        for c in range(CHUNKS)
    ]
    for copy in load_q:
        copy.start()

    barrier = pltpu.get_barrier_semaphore()
    for o in range(1, insts):
        pl.semaphore_signal(
            barrier, inc=1, device_id={"inst": lax.rem(me + o, insts)}, device_id_type=MESH
        )
    for t in range(1, tps, 2):
        pl.semaphore_signal(
            barrier, inc=1, device_id={"section": before, "tp": t}, device_id_type=MESH
        )

    @pl.when(merges)
    def _():
        for o in range(insts):
            pl.semaphore_signal(
                barrier,
                inc=1,
                device_id={"inst": lax.rem(me + o, insts), "tp": tp - 1},
                device_id_type=MESH,
            )

    load_fresh = pltpu.make_async_copy(fresh_hbm, fresh, load_sem.at[CHUNKS])
    load_len = pltpu.make_async_copy(len_hbm, length, load_sem.at[CHUNKS + 1])
    load_table = pltpu.make_async_copy(table_hbm, table, load_sem.at[CHUNKS + 2])
    parts = kv_sem.shape[0]
    per = pool // parts
    load_kv = [
        pltpu.make_async_copy(
            kv_hbm.at[pl.ds(c * per, per)], kv.at[pl.ds(c * per, per)], kv_sem.at[c]
        )
        for c in range(parts)
    ]
    for copy in [load_table, load_len, load_fresh] + load_kv:
        copy.start()

    @pl.when(merges)
    def _():
        pl.semaphore_wait(barrier, others + tps)

    @pl.when(jnp.logical_not(merges))
    def _():
        pl.semaphore_wait(barrier, others + insts)


    for c in range(CHUNKS):
        load_q[c].wait()
        for o in ORDER:
            copy = pltpu.make_async_remote_copy(
                src_ref=q_all.at[c, my_rows],
                dst_ref=q_all.at[c, my_rows],
                send_sem=q_ssem.at[c],
                recv_sem=q_rsem.at[c],
                device_id={"inst": lax.rem(me + o, insts)},
                device_id_type=MESH,
            )
            copy.start()

    load_len.wait()
    load_table.wait()
    page_id = iota((pool, rows), 0)
    counted = jnp.zeros((pool, rows), jnp.int32)
    for k in range(slots):
        local = table[k] - me * pool
        live = jnp.clip(length[...] - k * page, 0, page)
        counted = counted + jnp.where(page_id == local, live, 0)
    owned = counted > 0
    owner_f = jnp.where(owned, 1.0, 0.0).astype(F32)
    owner = owner_f.astype(BF16)
    owner_t = owner_f.T.astype(BF16)
    owner_t2 = jnp.concatenate([owner_t, owner_t], axis=1)
    token_buf[...] = dot(counted.astype(F32).astype(BF16), jnp.ones((rows, 128), BF16))

    load_fresh.wait()
    fresh_f[...] = fresh[...].astype(F32)
    own_k = fresh_f[pl.ds(0, home, stride=2), :]
    own_v = fresh_f[pl.ds(1, home, stride=2), :]
    lane = iota((home, 128), 1)
    own = jnp.zeros((home, 128), F32)
    for c in range(CHUNKS):
        q_mine = q_all[c, my_rows, :].astype(F32)
        for h in range(span):
            score = jnp.sum(q_mine[:, h * 128 : (h + 1) * 128] * own_k, axis=1, keepdims=True)
            own = jnp.where(lane == c * span + h, score * scale, own)

    own_send[0] = own
    own_send[1] = own_v

    @pl.when(jnp.logical_not(merges))
    def _():
        pltpu.make_async_remote_copy(
            src_ref=own_send,
            dst_ref=own_recv,
            send_sem=own_sem.at[0],
            recv_sem=own_sem.at[1],
            device_id={"tp": merger},
            device_id_type=MESH,
        ).start()

    for i in range(parts):
        load_kv[i].wait()
        for g in range(i * per // GROUP, (i + 1) * per // GROUP):
            at = slice(g * GROUP, (g + 1) * GROUP)
            keys[g] = kv[at, 0].reshape(GROUP * page, 128).T

    stack = span * GROUP
    groups = pool // GROUP
    row_page = lax.rem(iota((stack, 128), 0), GROUP)
    per_tile = 128 // page
    tiles = GROUP // per_tile
    tile_of = row_page // per_tile
    token = iota((stack, 128), 1) - lax.rem(row_page, per_tile) * page
    token_f = token.astype(F32)
    pool_lane = iota((pool, 128), 1)
    row_lane = iota((rows, 128), 1)
    def wait_q(c):
        arrived(q_all.at[c, pl.ds(0, others * home)], q_rsem.at[c])

    def pick(c):
        picked_buf[c] = dot(owner, q_all[c])

    def score_group(c, g, carry):
        at = pl.ds(pl.multiple_of(g * GROUP, GROUP), GROUP)
        group_q = jnp.concatenate(
            [picked_buf[c, at, h * 128 : (h + 1) * 128] for h in range(span)], axis=0
        ).astype(BF16)
        full = dot(group_q, keys[g])
        scores = full[:, :128]
        for i in range(1, tiles):
            scores = jnp.where(tile_of == i, full[:, i * 128 : (i + 1) * 128], scores)
        score_buf[c, g] = scores
        return carry

    def weigh_group(c, g, carry):
        at = pl.ds(pl.multiple_of(g * GROUP, GROUP), GROUP)
        limit = jnp.concatenate([token_buf[at, :]] * span, axis=0)
        valid = (token >= 0) & (token_f < limit)
        scores = jnp.where(valid, score_buf[c, g] * scale, NEGATIVE)
        highest = jnp.max(scores, axis=1, keepdims=True)
        weights = jnp.where(valid, jnp.exp(scores - highest), 0.0)
        total = jnp.sum(weights, axis=1, keepdims=True)
        weight_buf[c, g] = weights
        page_m[c, :, at, :] = jnp.broadcast_to(highest, (stack, 128)).reshape(span, GROUP, 128)
        page_s[c, :, at, :] = jnp.broadcast_to(total, (stack, 128)).reshape(span, GROUP, 128)
        return carry

    def value_group(c, g, carry):
        at = pl.ds(pl.multiple_of(g * GROUP, GROUP), GROUP)
        weights = weight_buf[c, g]
        spread = jnp.concatenate(
            [jnp.where(tile_of == i, weights, 0.0).astype(BF16) for i in range(tiles)], axis=1
        )
        x = dot(spread, kv[at, 1].reshape(GROUP * page, 128))
        page_x[c, :, at, :] = x.reshape(span, GROUP, 128)
        return carry

    def groupwise(body, c):
        lax.fori_loop(0, groups, functools.partial(body, c), 0, unroll=groups)

    def combine(c):
        refs = []
        for h in range(span):
            rounded = page_m[c, h].astype(BF16).astype(F32)
            refs.append(jnp.max(jnp.where(owned, rounded, NEGATIVE), axis=0, keepdims=True))
        sums = jnp.zeros((pool, 128), F32)
        stat = jnp.concatenate(refs + [jnp.zeros((128 - span, rows), F32)], axis=0).T
        for h in range(0, span, 2):
            sides = []
            for j in (h, h + 1):
                page_ref = dot_nt(owner, jnp.broadcast_to(refs[j], (128, rows)).astype(BF16))
                factor = jnp.exp(page_m[c, j] - page_ref)
                sums = jnp.where(pool_lane == span + j, factor * page_s[c, j], sums)
                high, low = split(factor * page_x[c, j])
                sides.append(jnp.concatenate([high, low], axis=0))
            both = dot(owner_t2, jnp.concatenate(sides, axis=1))
            for j in range(2):
                x = both[:, j * 128 : (j + 1) * 128]
                largest = jnp.maximum(jnp.max(jnp.abs(x), axis=1, keepdims=True), TINY)
                code = jnp.round(x * (LEVELS / largest)).astype(jnp.int32).astype(jnp.int16)
                stat = jnp.where(row_lane == 2 * span + h + j, largest * (1.0 / LEVELS), stat)
                first = (h + j) * home
                for d in range(insts):
                    p_send[d, c, first : first + home, :] = code[d * home : (d + 1) * home]
        high, low = split(sums)
        stat = stat + dot(owner_t2, jnp.concatenate([high, low], axis=0))
        for d in range(insts):
            s_send[d, c] = stat[d * home : (d + 1) * home]

    def send(c):
        def send_to(o, slot):
            to = lax.rem(me + o, insts)
            for src, dst, ssem, rsem in (
                (s_send, s_recv, s_ssem, s_rsem),
                (p_send, p_recv, p_ssem, p_rsem),
            ):
                pltpu.make_async_remote_copy(
                    src_ref=src.at[to, c],
                    dst_ref=dst.at[c, slot],
                    send_sem=ssem.at[c],
                    recv_sem=rsem.at[c, core],
                    device_id={"inst": to, "tp": merger},
                    device_id_type=MESH,
                ).start()

        for o in ORDER:
            send_to(o, o - 1 + core * others)

        @pl.when(jnp.logical_not(merges))
        def _():
            send_to(0, 2 * others)

    wait_q(0)
    pick(0)
    groupwise(score_group, 0)
    groupwise(weigh_group, 0)
    groupwise(value_group, 0)
    combine(0)
    send(0)
    wait_q(1)
    pick(1)
    groupwise(score_group, 1)
    groupwise(weigh_group, 1)
    groupwise(value_group, 1)
    combine(1)
    send(1)

    lower = iota((8, 128), 0) < part
    half = span * part

    def merge(c, k, own, own_v, stats, codes):
        mine = pltpu.roll(own, 128 - c * span, 1) if c else own
        highest = mine
        for s in stats:
            highest = jnp.maximum(highest, s)
        own_factor = jnp.exp(mine - highest)
        total = own_factor
        factors = []
        for s in stats:
            f = jnp.exp(s - highest)
            total = total + f * pltpu.roll(s, 128 - span, 1)
            factors.append(f * pltpu.roll(s, 128 - 2 * span, 1))
        inverse = 1.0 / total
        own_factor = own_factor * inverse
        factors = [f * inverse for f in factors]
        merged = []
        for h in range(span):
            at = slice(h * home, (h + 1) * home)
            acc = own_factor[:, h : h + 1] * own_v
            for f, code in zip(factors, codes):
                acc = acc + f[:, h : h + 1] * code(at).astype(F32)
            merged.append(acc)
        for u in range(home // 8):
            first, second = [], []
            for h in range(0, span, 2):
                a = merged[h][u * 8 : (u + 1) * 8]
                b = merged[h + 1][u * 8 : (u + 1) * 8]
                first.append(jnp.where(lower, a, pltpu.roll(b, part, 0)))
                second.append(jnp.where(lower, pltpu.roll(a, part, 0), b))
            r_send[c, k, 2 * u] = jnp.concatenate(first, axis=0).astype(BF16)
            r_send[c, k, 2 * u + 1] = jnp.concatenate(second, axis=0).astype(BF16)

    def send_rows(c, k):
        for t in range(tps):
            pltpu.make_async_remote_copy(
                src_ref=r_send.at[c, k, t],
                dst_ref=out_ref.at[tp - 1 + k, pl.ds(c * half, half)],
                send_sem=r_ssem.at[c],
                recv_sem=r_rsem.at[c],
                device_id={"section": after, "tp": t},
                device_id_type=MESH,
            ).start()

    @pl.when(merges)
    def _():
        for c in range(CHUNKS):
            received = [lambda at, c=c, o=o: p_recv[c, o, at, :] for o in range(2 * others + 1)]
            near = [o for o in range(others)] + [2 * others]
            far = [o + others for o in range(others)]
            arrived(s_recv.at[c, pl.ds(0, others)], s_rsem.at[c, 1])
            arrived(p_recv.at[c, pl.ds(0, others)], p_rsem.at[c, 1])
            merge(
                c,
                1,
                own_send[0],
                own_send[1],
                [s_send[me, c]] + [s_recv[c, o] for o in far],
                [lambda at, c=c: p_send[me, c, at, :]] + [received[o] for o in far],
            )
            send_rows(c, 1)
            if c == 0:
                arrived(own_recv, own_sem.at[1])
            arrived(s_recv.at[c, pl.ds(0, insts)], s_rsem.at[c, 0])
            arrived(p_recv.at[c, pl.ds(0, insts)], p_rsem.at[c, 0])
            merge(
                c,
                0,
                own_recv[0],
                own_recv[1],
                [s_recv[c, o] for o in near],
                [received[o] for o in near],
            )
            send_rows(c, 0)
        for c in range(CHUNKS):
            arrived(s_recv.at[c, pl.ds(0, others)], s_ssem.at[c])
            arrived(p_recv.at[c, pl.ds(0, others)], p_ssem.at[c])
            arrived(r_send.at[c], r_ssem.at[c])

    @pl.when(jnp.logical_not(merges))
    def _():
        arrived(own_send, own_sem.at[0])
        for c in range(CHUNKS):
            arrived(s_recv.at[c, pl.ds(0, insts)], s_ssem.at[c])
            arrived(p_recv.at[c, pl.ds(0, insts)], p_ssem.at[c])

    for c in range(CHUNKS):
        arrived(q_all.at[c, pl.ds(0, others * home)], q_ssem.at[c])
    for c in range(CHUNKS):
        arrived(r_send.at[c, 0], r_rsem.at[c])


def shards(queries, new_kv, kv_pages, lengths, block_tables):
    sections = lax.axis_size("section")
    insts = lax.axis_size("inst")
    tps = lax.axis_size("tp")
    home = queries.shape[1]
    heads = queries.shape[2] // HEAD_DIM
    pool, page = kv_pages.shape[1], kv_pages.shape[3]
    rows, slots = block_tables.shape[1:]
    part = home // tps
    sizes = (sections, insts, tps, home, pool, slots, page, heads)
    others = insts - 1
    span = heads // CHUNKS
    groups, stack, wide = pool // GROUP, span * GROUP, span * home
    out = pl.pallas_call(
        functools.partial(kernel, sizes),
        out_shape=pltpu.VMEM((tps, heads * part, HEAD_DIM), BF16),
        in_specs=[pl.BlockSpec(memory_space=pltpu.HBM)] * 5,
        out_specs=pl.BlockSpec(memory_space=pltpu.VMEM),
        scratch_shapes=[
            pltpu.VMEM((CHUNKS, rows, span * HEAD_DIM), BF16),
            pltpu.VMEM((2 * home, HEAD_DIM), BF16),
            pltpu.VMEM((2 * home, HEAD_DIM), F32),
            pltpu.VMEM((pool, 2, page, HEAD_DIM), BF16),
            pltpu.VMEM((groups, HEAD_DIM, GROUP * page), BF16),
            pltpu.VMEM((1, rows), jnp.int32),
            pltpu.VMEM((slots, 1, rows), jnp.int32),
            pltpu.VMEM((CHUNKS, pool, span * HEAD_DIM), F32),
            pltpu.VMEM((pool, 128), F32),
            pltpu.VMEM((CHUNKS, groups, stack, 128), F32),
            pltpu.VMEM((CHUNKS, groups, stack, 128), F32),
            pltpu.VMEM((CHUNKS, span, pool, HEAD_DIM), F32),
            pltpu.VMEM((CHUNKS, span, pool, HEAD_DIM), F32),
            pltpu.VMEM((CHUNKS, span, pool, HEAD_DIM), F32),
            pltpu.VMEM((insts, CHUNKS, wide, HEAD_DIM), jnp.int16),
            pltpu.VMEM((CHUNKS, 2 * others + 1, wide, HEAD_DIM), jnp.int16),
            pltpu.VMEM((insts, CHUNKS, home, 128), F32),
            pltpu.VMEM((CHUNKS, 2 * others + 1, home, 128), F32),
            pltpu.VMEM((CHUNKS, 2, tps, span * part, HEAD_DIM), BF16),
            pltpu.VMEM((2, home, 128), F32),
            pltpu.VMEM((2, home, 128), F32),
            pltpu.SemaphoreType.DMA((CHUNKS + 3,)),
            pltpu.SemaphoreType.DMA((4,)),
            pltpu.SemaphoreType.DMA((CHUNKS,)),
            pltpu.SemaphoreType.DMA((CHUNKS,)),
            pltpu.SemaphoreType.DMA((CHUNKS,)),
            pltpu.SemaphoreType.DMA((CHUNKS, 2)),
            pltpu.SemaphoreType.DMA((CHUNKS,)),
            pltpu.SemaphoreType.DMA((CHUNKS, 2)),
            pltpu.SemaphoreType.DMA((CHUNKS,)),
            pltpu.SemaphoreType.DMA((CHUNKS,)),
            pltpu.SemaphoreType.DMA((2,)),
        ],
        compiler_params=pltpu.CompilerParams(
            collective_id=0, has_side_effects=True, vmem_limit_bytes=32 * 1024 * 1024
        ),
    )(
        *(
            pltpu.with_memory_space_constraint(x, pltpu.HBM)
            for x in (
                queries[0],
                new_kv[0].reshape(2 * home, HEAD_DIM),
                kv_pages[0],
                lengths,
                jnp.transpose(block_tables, (2, 0, 1)),
            )
        )
    )
    out = out.reshape(tps, heads, part, HEAD_DIM).transpose(2, 0, 1, 3)
    return out.reshape(1, part, tps * heads * HEAD_DIM)


def solution(mesh):
    placed = (
        P("section", "inst", "tp"),
        P("section", "inst", None, "tp"),
        P("section", "inst", None, None, "tp"),
        P("section", None),
        P("section", None, None),
    )
    return jax.shard_map(
        shards,
        mesh=mesh,
        in_specs=placed,
        out_specs=P("section", ("inst", "tp"), None),
        check_vma=False,
    )
```

```python
import functools
import math

import jax
import jax.numpy as jnp
from jax import lax
from jax.experimental import pallas as pl
from jax.experimental.pallas import tpu as pltpu
from jax.sharding import PartitionSpec as P

HEAD_DIM = 128
NEGATIVE = -1e30
GROUP = 8
CHUNKS = 2
ORDER = (2, 1, 3)
LEVELS = 32767.0
TINY = 1e-30
MESH = pl.DeviceIdType.MESH
F32 = jnp.float32
BF16 = jnp.bfloat16


def iota(shape, dim):
    return lax.broadcasted_iota(jnp.int32, shape, dim)


def dot(a, b):
    return lax.dot_general(a, b, (((1,), (0,)), ((), ())), preferred_element_type=F32)


def dot_nt(a, b):
    return lax.dot_general(a, b, (((1,), (1,)), ((), ())), preferred_element_type=F32)


def split(x):
    high = x.astype(BF16)
    return high, (x - high.astype(F32)).astype(BF16)


def arrived(ref, sem):
    pltpu.make_async_copy(ref, ref, sem).wait()


def kernel(
    sizes,
    q_hbm,
    fresh_hbm,
    kv_hbm,
    len_hbm,
    table_hbm,
    out_ref,
    q_all,
    fresh,
    fresh_f,
    kv,
    keys,
    length,
    table,
    picked_buf,
    token_buf,
    score_buf,
    weight_buf,
    page_x,
    page_m,
    page_s,
    p_send,
    p_recv,
    s_send,
    s_recv,
    r_send,
    own_send,
    own_recv,
    load_sem,
    kv_sem,
    q_ssem,
    q_rsem,
    p_ssem,
    p_rsem,
    s_ssem,
    s_rsem,
    r_ssem,
    r_rsem,
    own_sem,
):
    sections, insts, tps, home, pool, slots, page, heads = sizes
    rows = home * insts
    part = home // tps
    scale = 1.0 / math.sqrt(HEAD_DIM)
    sec = lax.axis_index("section")
    me = lax.axis_index("inst")
    tp = lax.axis_index("tp")
    core = lax.rem(tp, 2)
    merger = tp + 1 - core
    merges = core == 1
    others = insts - 1
    before = lax.rem(sec + sections - 1, sections)
    after = lax.rem(sec + 1, sections)
    my_rows = pl.ds(pl.multiple_of(me * home, home), home)

    span = heads // CHUNKS
    width = span * HEAD_DIM
    load_q = [
        pltpu.make_async_copy(
            q_hbm.at[:, pl.ds(c * width, width)], q_all.at[c, my_rows], load_sem.at[c]
        )
        for c in range(CHUNKS)
    ]
    for copy in load_q:
        copy.start()

    barrier = pltpu.get_barrier_semaphore()
    for o in range(1, insts):
        pl.semaphore_signal(
            barrier, inc=1, device_id={"inst": lax.rem(me + o, insts)}, device_id_type=MESH
        )
    for t in range(1, tps, 2):
        pl.semaphore_signal(
            barrier, inc=1, device_id={"section": before, "tp": t}, device_id_type=MESH
        )

    @pl.when(merges)
    def _():
        for o in range(insts):
            pl.semaphore_signal(
                barrier,
                inc=1,
                device_id={"inst": lax.rem(me + o, insts), "tp": tp - 1},
                device_id_type=MESH,
            )

    load_fresh = pltpu.make_async_copy(fresh_hbm, fresh, load_sem.at[CHUNKS])
    load_len = pltpu.make_async_copy(len_hbm, length, load_sem.at[CHUNKS + 1])
    load_table = pltpu.make_async_copy(table_hbm, table, load_sem.at[CHUNKS + 2])
    parts = kv_sem.shape[0]
    per = pool // parts
    load_kv = [
        pltpu.make_async_copy(
            kv_hbm.at[pl.ds(c * per, per)], kv.at[pl.ds(c * per, per)], kv_sem.at[c]
        )
        for c in range(parts)
    ]
    for copy in [load_table, load_len, load_fresh] + load_kv:
        copy.start()

    @pl.when(merges)
    def _():
        pl.semaphore_wait(barrier, others + tps)

    @pl.when(jnp.logical_not(merges))
    def _():
        pl.semaphore_wait(barrier, others + insts)


    for c in range(CHUNKS):
        load_q[c].wait()
        for o in ORDER:
            copy = pltpu.make_async_remote_copy(
                src_ref=q_all.at[c, my_rows],
                dst_ref=q_all.at[c, my_rows],
                send_sem=q_ssem.at[c],
                recv_sem=q_rsem.at[c],
                device_id={"inst": lax.rem(me + o, insts)},
                device_id_type=MESH,
            )
            copy.start()

    load_len.wait()
    load_table.wait()
    page_id = iota((pool, rows), 0)
    counted = jnp.zeros((pool, rows), jnp.int32)
    for k in range(slots):
        local = table[k] - me * pool
        live = jnp.clip(length[...] - k * page, 0, page)
        counted = counted + jnp.where(page_id == local, live, 0)
    owned = counted > 0
    owner_f = jnp.where(owned, 1.0, 0.0).astype(F32)
    owner = owner_f.astype(BF16)
    owner_t = owner_f.T.astype(BF16)
    owner_t2 = jnp.concatenate([owner_t, owner_t], axis=1)
    token_buf[...] = dot(counted.astype(F32).astype(BF16), jnp.ones((rows, 128), BF16))

    load_fresh.wait()
    fresh_f[...] = fresh[...].astype(F32)
    own_k = fresh_f[pl.ds(0, home, stride=2), :]
    own_v = fresh_f[pl.ds(1, home, stride=2), :]
    lane = iota((home, 128), 1)
    own = jnp.zeros((home, 128), F32)
    for c in range(CHUNKS):
        q_mine = q_all[c, my_rows, :].astype(F32)
        for h in range(span):
            score = jnp.sum(q_mine[:, h * 128 : (h + 1) * 128] * own_k, axis=1, keepdims=True)
            own = jnp.where(lane == c * span + h, score * scale, own)

    own_send[0] = own
    own_send[1] = own_v

    @pl.when(jnp.logical_not(merges))
    def _():
        pltpu.make_async_remote_copy(
            src_ref=own_send,
            dst_ref=own_recv,
            send_sem=own_sem.at[0],
            recv_sem=own_sem.at[1],
            device_id={"tp": merger},
            device_id_type=MESH,
        ).start()

    for i in range(parts):
        load_kv[i].wait()
        for g in range(i * per // GROUP, (i + 1) * per // GROUP):
            at = slice(g * GROUP, (g + 1) * GROUP)
            keys[g] = kv[at, 0].reshape(GROUP * page, 128).T

    stack = span * GROUP
    groups = pool // GROUP
    row_page = lax.rem(iota((stack, 128), 0), GROUP)
    per_tile = 128 // page
    tiles = GROUP // per_tile
    tile_of = row_page // per_tile
    token = iota((stack, 128), 1) - lax.rem(row_page, per_tile) * page
    token_f = token.astype(F32)
    pool_lane = iota((pool, 128), 1)
    row_lane = iota((rows, 128), 1)
    def wait_q(c):
        arrived(q_all.at[c, pl.ds(0, others * home)], q_rsem.at[c])

    def pick(c):
        picked_buf[c] = dot(owner, q_all[c])

    def score_group(c, g, carry):
        at = pl.ds(pl.multiple_of(g * GROUP, GROUP), GROUP)
        group_q = jnp.concatenate(
            [picked_buf[c, at, h * 128 : (h + 1) * 128] for h in range(span)], axis=0
        ).astype(BF16)
        full = dot(group_q, keys[g])
        scores = full[:, :128]
        for i in range(1, tiles):
            scores = jnp.where(tile_of == i, full[:, i * 128 : (i + 1) * 128], scores)
        score_buf[c, g] = scores
        return carry

    def weigh_group(c, g, carry):
        at = pl.ds(pl.multiple_of(g * GROUP, GROUP), GROUP)
        limit = jnp.concatenate([token_buf[at, :]] * span, axis=0)
        valid = (token >= 0) & (token_f < limit)
        scores = jnp.where(valid, score_buf[c, g] * scale, NEGATIVE)
        highest = jnp.max(scores, axis=1, keepdims=True)
        weights = jnp.where(valid, jnp.exp(scores - highest), 0.0)
        total = jnp.sum(weights, axis=1, keepdims=True)
        weight_buf[c, g] = weights
        page_m[c, :, at, :] = jnp.broadcast_to(highest, (stack, 128)).reshape(span, GROUP, 128)
        page_s[c, :, at, :] = jnp.broadcast_to(total, (stack, 128)).reshape(span, GROUP, 128)
        return carry

    def value_group(c, g, carry):
        at = pl.ds(pl.multiple_of(g * GROUP, GROUP), GROUP)
        weights = weight_buf[c, g]
        spread = jnp.concatenate(
            [jnp.where(tile_of == i, weights, 0.0).astype(BF16) for i in range(tiles)], axis=1
        )
        x = dot(spread, kv[at, 1].reshape(GROUP * page, 128))
        page_x[c, :, at, :] = x.reshape(span, GROUP, 128)
        return carry

    def groupwise(body, c):
        lax.fori_loop(0, groups, functools.partial(body, c), 0, unroll=groups)

    lanes = 128 // (home // 8)

    def unpack(block):
        return jnp.concatenate(
            [block] + [pltpu.roll(block, 128 - i * lanes, 1) for i in range(1, home // 8)], axis=0
        )

    def combine(c):
        refs = []
        for h in range(span):
            rounded = page_m[c, h].astype(BF16).astype(F32)
            refs.append(jnp.max(jnp.where(owned, rounded, NEGATIVE), axis=0, keepdims=True))
        sums = jnp.zeros((pool, 128), F32)
        stat = jnp.concatenate(refs + [jnp.zeros((128 - span, rows), F32)], axis=0).T
        for h in range(0, span, 2):
            sides = []
            for j in (h, h + 1):
                page_ref = dot_nt(owner, jnp.broadcast_to(refs[j], (128, rows)).astype(BF16))
                factor = jnp.exp(page_m[c, j] - page_ref)
                sums = jnp.where(pool_lane == span + j, factor * page_s[c, j], sums)
                high, low = split(factor * page_x[c, j])
                sides.append(jnp.concatenate([high, low], axis=0))
            both = dot(owner_t2, jnp.concatenate(sides, axis=1))
            for j in range(2):
                x = both[:, j * 128 : (j + 1) * 128]
                largest = jnp.maximum(jnp.max(jnp.abs(x), axis=1, keepdims=True), TINY)
                code = jnp.round(x * (LEVELS / largest)).astype(jnp.int32).astype(jnp.int16)
                stat = jnp.where(row_lane == 2 * span + h + j, largest * (1.0 / LEVELS), stat)
                first = (h + j) * home
                for d in range(insts):
                    p_send[d, c, first : first + home, :] = code[d * home : (d + 1) * home]
        high, low = split(sums)
        stat = stat + dot(owner_t2, jnp.concatenate([high, low], axis=0))
        for d in range(insts):
            block = stat[d * home : d * home + 8]
            for i in range(1, home // 8):
                first = d * home + 8 * i
                block = block + pltpu.roll(stat[first : first + 8], i * lanes, 1)
            s_send[d, c] = block

    def send(c):
        def send_to(o, slot):
            to = lax.rem(me + o, insts)
            for src, dst, ssem, rsem in (
                (s_send, s_recv, s_ssem, s_rsem),
                (p_send, p_recv, p_ssem, p_rsem),
            ):
                pltpu.make_async_remote_copy(
                    src_ref=src.at[to, c],
                    dst_ref=dst.at[c, slot],
                    send_sem=ssem.at[c],
                    recv_sem=rsem.at[c, core],
                    device_id={"inst": to, "tp": merger},
                    device_id_type=MESH,
                ).start()

        for o in ORDER:
            send_to(o, o - 1 + core * others)

        @pl.when(jnp.logical_not(merges))
        def _():
            send_to(0, 2 * others)

    wait_q(0)
    pick(0)
    groupwise(score_group, 0)
    groupwise(weigh_group, 0)
    groupwise(value_group, 0)
    combine(0)
    send(0)
    wait_q(1)
    pick(1)
    groupwise(score_group, 1)
    groupwise(weigh_group, 1)
    groupwise(value_group, 1)
    combine(1)
    send(1)

    lower = iota((8, 128), 0) < part
    half = span * part

    def merge(c, k, own, own_v, stats, codes):
        mine = pltpu.roll(own, 128 - c * span, 1) if c else own
        highest = mine
        for s in stats:
            highest = jnp.maximum(highest, s)
        own_factor = jnp.exp(mine - highest)
        total = own_factor
        factors = []
        for s in stats:
            f = jnp.exp(s - highest)
            total = total + f * pltpu.roll(s, 128 - span, 1)
            factors.append(f * pltpu.roll(s, 128 - 2 * span, 1))
        inverse = 1.0 / total
        own_factor = own_factor * inverse
        factors = [f * inverse for f in factors]
        merged = []
        for h in range(span):
            at = slice(h * home, (h + 1) * home)
            acc = own_factor[:, h : h + 1] * own_v
            for f, code in zip(factors, codes):
                acc = acc + f[:, h : h + 1] * code(at).astype(F32)
            merged.append(acc)
        for u in range(home // 8):
            first, second = [], []
            for h in range(0, span, 2):
                a = merged[h][u * 8 : (u + 1) * 8]
                b = merged[h + 1][u * 8 : (u + 1) * 8]
                first.append(jnp.where(lower, a, pltpu.roll(b, part, 0)))
                second.append(jnp.where(lower, pltpu.roll(a, part, 0), b))
            r_send[c, k, 2 * u] = jnp.concatenate(first, axis=0).astype(BF16)
            r_send[c, k, 2 * u + 1] = jnp.concatenate(second, axis=0).astype(BF16)

    def send_rows(c, k):
        for t in range(tps):
            pltpu.make_async_remote_copy(
                src_ref=r_send.at[c, k, t],
                dst_ref=out_ref.at[tp - 1 + k, pl.ds(c * half, half)],
                send_sem=r_ssem.at[c],
                recv_sem=r_rsem.at[c],
                device_id={"section": after, "tp": t},
                device_id_type=MESH,
            ).start()

    @pl.when(merges)
    def _():
        for c in range(CHUNKS):
            received = [lambda at, c=c, o=o: p_recv[c, o, at, :] for o in range(2 * others + 1)]
            near = [o for o in range(others)] + [2 * others]
            far = [o + others for o in range(others)]
            arrived(s_recv.at[c, pl.ds(0, others)], s_rsem.at[c, 1])
            arrived(p_recv.at[c, pl.ds(0, others)], p_rsem.at[c, 1])
            merge(
                c,
                1,
                own_send[0],
                own_send[1],
                [unpack(s_send[me, c])] + [unpack(s_recv[c, o]) for o in far],
                [lambda at, c=c: p_send[me, c, at, :]] + [received[o] for o in far],
            )
            send_rows(c, 1)
            if c == 0:
                arrived(own_recv, own_sem.at[1])
            arrived(s_recv.at[c, pl.ds(0, insts)], s_rsem.at[c, 0])
            arrived(p_recv.at[c, pl.ds(0, insts)], p_rsem.at[c, 0])
            merge(
                c,
                0,
                own_recv[0],
                own_recv[1],
                [unpack(s_recv[c, o]) for o in near],
                [received[o] for o in near],
            )
            send_rows(c, 0)
        for c in range(CHUNKS):
            arrived(s_recv.at[c, pl.ds(0, others)], s_ssem.at[c])
            arrived(p_recv.at[c, pl.ds(0, others)], p_ssem.at[c])
            arrived(r_send.at[c], r_ssem.at[c])

    @pl.when(jnp.logical_not(merges))
    def _():
        arrived(own_send, own_sem.at[0])
        for c in range(CHUNKS):
            arrived(s_recv.at[c, pl.ds(0, insts)], s_ssem.at[c])
            arrived(p_recv.at[c, pl.ds(0, insts)], p_ssem.at[c])

    for c in range(CHUNKS):
        arrived(q_all.at[c, pl.ds(0, others * home)], q_ssem.at[c])
    for c in range(CHUNKS):
        arrived(r_send.at[c, 0], r_rsem.at[c])


def shards(queries, new_kv, kv_pages, lengths, block_tables):
    sections = lax.axis_size("section")
    insts = lax.axis_size("inst")
    tps = lax.axis_size("tp")
    home = queries.shape[1]
    heads = queries.shape[2] // HEAD_DIM
    pool, page = kv_pages.shape[1], kv_pages.shape[3]
    rows, slots = block_tables.shape[1:]
    part = home // tps
    sizes = (sections, insts, tps, home, pool, slots, page, heads)
    others = insts - 1
    span = heads // CHUNKS
    groups, stack, wide = pool // GROUP, span * GROUP, span * home
    out = pl.pallas_call(
        functools.partial(kernel, sizes),
        out_shape=pltpu.VMEM((tps, heads * part, HEAD_DIM), BF16),
        in_specs=[pl.BlockSpec(memory_space=pltpu.HBM)] * 5,
        out_specs=pl.BlockSpec(memory_space=pltpu.VMEM),
        scratch_shapes=[
            pltpu.VMEM((CHUNKS, rows, span * HEAD_DIM), BF16),
            pltpu.VMEM((2 * home, HEAD_DIM), BF16),
            pltpu.VMEM((2 * home, HEAD_DIM), F32),
            pltpu.VMEM((pool, 2, page, HEAD_DIM), BF16),
            pltpu.VMEM((groups, HEAD_DIM, GROUP * page), BF16),
            pltpu.VMEM((1, rows), jnp.int32),
            pltpu.VMEM((slots, 1, rows), jnp.int32),
            pltpu.VMEM((CHUNKS, pool, span * HEAD_DIM), F32),
            pltpu.VMEM((pool, 128), F32),
            pltpu.VMEM((CHUNKS, groups, stack, 128), F32),
            pltpu.VMEM((CHUNKS, groups, stack, 128), F32),
            pltpu.VMEM((CHUNKS, span, pool, HEAD_DIM), F32),
            pltpu.VMEM((CHUNKS, span, pool, HEAD_DIM), F32),
            pltpu.VMEM((CHUNKS, span, pool, HEAD_DIM), F32),
            pltpu.VMEM((insts, CHUNKS, wide, HEAD_DIM), jnp.int16),
            pltpu.VMEM((CHUNKS, 2 * others + 1, wide, HEAD_DIM), jnp.int16),
            pltpu.VMEM((insts, CHUNKS, 8, 128), F32),
            pltpu.VMEM((CHUNKS, 2 * others + 1, 8, 128), F32),
            pltpu.VMEM((CHUNKS, 2, tps, span * part, HEAD_DIM), BF16),
            pltpu.VMEM((2, home, 128), F32),
            pltpu.VMEM((2, home, 128), F32),
            pltpu.SemaphoreType.DMA((CHUNKS + 3,)),
            pltpu.SemaphoreType.DMA((4,)),
            pltpu.SemaphoreType.DMA((CHUNKS,)),
            pltpu.SemaphoreType.DMA((CHUNKS,)),
            pltpu.SemaphoreType.DMA((CHUNKS,)),
            pltpu.SemaphoreType.DMA((CHUNKS, 2)),
            pltpu.SemaphoreType.DMA((CHUNKS,)),
            pltpu.SemaphoreType.DMA((CHUNKS, 2)),
            pltpu.SemaphoreType.DMA((CHUNKS,)),
            pltpu.SemaphoreType.DMA((CHUNKS,)),
            pltpu.SemaphoreType.DMA((2,)),
        ],
        compiler_params=pltpu.CompilerParams(
            collective_id=0, has_side_effects=True, vmem_limit_bytes=32 * 1024 * 1024
        ),
    )(
        *(
            pltpu.with_memory_space_constraint(x, pltpu.HBM)
            for x in (
                queries[0],
                new_kv[0].reshape(2 * home, HEAD_DIM),
                kv_pages[0],
                lengths,
                jnp.transpose(block_tables, (2, 0, 1)),
            )
        )
    )
    out = out.reshape(tps, heads, part, HEAD_DIM).transpose(2, 0, 1, 3)
    return out.reshape(1, part, tps * heads * HEAD_DIM)


def solution(mesh):
    placed = (
        P("section", "inst", "tp"),
        P("section", "inst", None, "tp"),
        P("section", "inst", None, None, "tp"),
        P("section", None),
        P("section", None, None),
    )
    return jax.shard_map(
        shards,
        mesh=mesh,
        in_specs=placed,
        out_specs=P("section", ("inst", "tp"), None),
        check_vma=False,
    )
```
